32 devices in a mesh: row: 8 (over z, y), col: 4 (over x, core).
Axes of the slice: x: 2, y: 2, z: 4, core: 2. Of those that a mesh axis runs over, the one named last changes fastest.
Arguments:
- amplitudes_right: float32 [8, 2048], P(None, ('row', 'col')), may hold values from -5 to 5
- amplitudes_left: float32 [8, 2048], P(None, ('row', 'col')), may hold values from -7 to 7
- previous_right: float32 [8, 2048], P(None, ('row', 'col')), may hold values from -6 to 6
- previous_left: float32 [8, 2048], P(None, ('row', 'col')), may hold values from -6 to 6
- coupling: float32 [2, 8], replicated, may hold values from 0.2 to 1
- ladder: bfloat16 [2048, 2048], P('row', 'col'), may hold values from -1 to 5
Outputs:
- next_right: float32 [8, 2048], P(None, ('row', 'col'))
- next_left: float32 [8, 2048], P(None, ('row', 'col'))
- coefficients: float32 [3, 8], replicated
The draws below stay inside these ranges and needn't reach their ends.
All inputs are finite; a program needn't handle non-finite values.
Results may differ from the reference program's by a relative error of at most 0.003.
Values may be sent and summed in bfloat16 or wider, within the bound.
A program may use at most 64 MiB of HBM per device.

```python
import jax
import jax.numpy as jnp
from jax import lax

COLS = 8
PAIRS = 2048


def shared_base(key):
    return jnp.clip(jax.random.normal(jax.random.fold_in(key, 11), (COLS, PAIRS), jnp.float32), -5.0, 5.0)


def draw_amplitudes_right(key, part):
    base = shared_base(key)
    return base


def draw_amplitudes_left(key, part):
    base = shared_base(key)
    key = jax.random.fold_in(key, 2)
    key_mix, key_noise = jax.random.split(key)
    mixing = jax.random.uniform(key_mix, (COLS, 1), jnp.float32, -0.6, 0.6)
    noise = jnp.clip(jax.random.normal(key_noise, (COLS, PAIRS), jnp.float32), -5.0, 5.0)
    return mixing * base + 0.8 * noise


def draw_ladder(key, part):
    key = jax.random.fold_in(key, 3)
    key_off, key_diag = jax.random.split(key)
    spread = jnp.clip(jax.random.normal(key_off, (PAIRS, PAIRS), jnp.float32), -5.0, 5.0)
    diagonal = jax.random.uniform(key_diag, (PAIRS,), jnp.float32, 1.0, 3.0)
    positions = jnp.arange(PAIRS)
    on_diag = positions[:, None] == positions[None, :]
    matrix = spread / jnp.sqrt(jnp.float32(PAIRS)) + jnp.where(on_diag, diagonal[:, None], 0.0)
    return matrix.astype(jnp.bfloat16)


def block_scale(key, shape, pieces, low, top_value):
    level = 1.0
    for axis_at, blocks in pieces:
        heights = jax.random.uniform(jax.random.fold_in(jax.random.fold_in(key, 6), axis_at), (blocks,), jnp.float32, low / len(pieces), top_value / len(pieces))
        level = level * jnp.repeat(jnp.exp(heights), shape[axis_at] // blocks).reshape((-1,) + (1,) * (len(shape) - 1 - axis_at))
    return level


def bell_draw(own_key, shape, deviation, most, cuts=(), held_as=jnp.bfloat16):
    array = deviation * jax.random.normal(own_key, shape, jnp.float32)
    if cuts:
        array = array * block_scale(own_key, shape, cuts, -0.22, 0.18)
    return jnp.clip(array, -most, most).astype(held_as)


def setup_inputs(seed: int = 0) -> dict:
    key_of = jax.random.split(jax.random.key(seed), 7)
    return {
        "amplitudes_right": draw_amplitudes_right(jax.random.fold_in(key_of[6], 71), 0),
        "amplitudes_left": draw_amplitudes_left(jax.random.fold_in(key_of[6], 71), 0),
        "previous_right": bell_draw(key_of[2], (COLS, PAIRS), 1.0, 6.0, ((1, 32),), jnp.float32),
        "previous_left": bell_draw(key_of[3], (COLS, PAIRS), 1.0, 6.0, ((1, 32),), jnp.float32),
        "coupling": jnp.clip(jax.random.uniform(key_of[4], (2, COLS), jnp.float32, 0.2, 1.0), 0.2, 1.0),
        "ladder": draw_ladder(jax.random.fold_in(key_of[6], 71), 0),
    }


def inner_mean(first, second):
    return lax.optimization_barrier(jnp.sum(first * second, axis=1)) / PAIRS

def reference(amplitudes_right, amplitudes_left, previous_right, previous_left, coupling, ladder):
    right_half = amplitudes_right.astype(jnp.bfloat16)
    left_half = amplitudes_left.astype(jnp.bfloat16)
    image_right = lax.dot_general(right_half, ladder, (((1,), (1,)), ((), ())), preferred_element_type=jnp.float32)
    image_left = jnp.dot(left_half, ladder, preferred_element_type=jnp.float32)
    alpha_now = inner_mean(amplitudes_left, image_right)
    right_res = image_right - alpha_now[:, None] * amplitudes_right - coupling[1][:, None] * previous_right
    left_res = image_left - alpha_now[:, None] * amplitudes_left - coupling[0][:, None] * previous_left
    omega_val = inner_mean(left_res, right_res)
    right_norm = inner_mean(right_res, right_res)
    left_norm = inner_mean(left_res, left_res)
    safe_omega = jnp.maximum(jnp.abs(omega_val), 0.1 * jnp.sqrt(right_norm * left_norm + 1e-06))
    beta_new = jnp.sqrt(safe_omega)
    gamma_new = omega_val / beta_new
    next_right = right_res / beta_new[:, None]
    next_left = left_res * (gamma_new / safe_omega)[:, None]
    coefficients = jnp.stack([alpha_now, beta_new, gamma_new])
    return (next_right, next_left, coefficients)
```

```python
import functools

import jax
import jax.numpy as jnp
from jax import lax
from jax.experimental import pallas as pl
from jax.experimental.pallas import tpu as pltpu
from jax.sharding import PartitionSpec as P

MESH = pl.DeviceIdType.MESH
LANES = 128
UNROLL_MOST = 32


def each(count, body):
    if count <= UNROLL_MOST:
        for i in range(count):
            body(i)
    else:
        lax.fori_loop(0, count, lambda i, carry: (body(i), carry)[1], 0)


def arrived(ref, count, sem):
    part = ref.at[pl.ds(0, count)]
    pltpu.make_async_copy(part, part, sem).wait()


def kernel(
    rows_count,
    cols_count,
    right_in,
    left_in,
    prev_right_in,
    prev_left_in,
    coupling_in,
    ladder_in,
    next_right_out,
    next_left_out,
    coefficients_out,
    right_own,
    left_own,
    prev_right_own,
    prev_left_own,
    coupling_own,
    ladder_own,
    right_sent,
    left_sent,
    right_got,
    left_got,
    right_part,
    left_part,
    right_part_got,
    left_part_got,
    alpha_sent,
    alpha_got,
    norms_sent,
    norms_got,
    load_sem,
    send_sem,
    recv_sem,
):
    devices = rows_count * cols_count
    depth, share = right_own.shape
    pack = LANES // share
    pairs_total = share * devices
    my_row = lax.axis_index("row")
    my_col = lax.axis_index("col")
    me = my_row * cols_count + my_col
    home_col = me // rows_count
    home_slot = lax.rem(me, rows_count)
    at_home = home_col == my_col

    loads = [
        pltpu.make_async_copy(src, dst, load_sem.at[i])
        for i, (src, dst) in enumerate(
            (
                (right_in, right_own),
                (left_in, left_own),
                (prev_right_in, prev_right_own),
                (prev_left_in, prev_left_own),
                (coupling_in, coupling_own),
                (ladder_in, ladder_own),
            )
        )
    ]
    for load in loads:
        load.start()

    def other(step):
        device = lax.rem(me + step + 1, devices)
        return (device // cols_count, lax.rem(device, cols_count))

    barrier = pltpu.get_barrier_semaphore()
    each(
        devices - 1,
        lambda i: pl.semaphore_signal(barrier, inc=1, device_id=other(i), device_id_type=MESH),
    )

    lane = lax.broadcasted_iota(jnp.int32, (depth, LANES), 1)
    sub = lax.broadcasted_iota(jnp.int32, (depth, LANES), 0)
    mine = lane // share == lax.rem(my_col, pack)

    def spread(array):
        return jnp.where(mine, jnp.concatenate([array] * pack, axis=1), 0.0)

    def to_lanes(columns):
        row = jnp.zeros((depth, LANES), jnp.float32)
        for i, column in enumerate(columns):
            row = row + jnp.where(lane == sub + i * depth, column, 0.0)
        return jnp.sum(row, axis=0, keepdims=True)

    def to_column(row, i):
        return jnp.sum(jnp.where(lane == sub + i * depth, row, 0.0), axis=1, keepdims=True)

    loads[0].wait()
    loads[1].wait()
    right = spread(right_own[...])
    left = spread(left_own[...])
    right_sent[0] = right
    left_sent[0] = left
    left_got[pl.ds(my_col, 1)] = left[None]

    @pl.when(at_home)
    def _():
        right_got[pl.ds(home_slot, 1)] = right[None]

    pl.semaphore_wait(barrier, devices - 1)

    def send_right(i):
        row = lax.rem(my_row + i, rows_count)

        def go():
            pltpu.make_async_remote_copy(
                src_ref=right_sent.at[0],
                dst_ref=right_got.at[home_slot],
                send_sem=send_sem.at[0],
                recv_sem=recv_sem.at[0],
                device_id=(row, home_col),
                device_id_type=MESH,
            ).start()

        if isinstance(i, int) and i > 0:
            go()
        else:
            pl.when(jnp.logical_or(row != my_row, home_col != my_col))(go)

    each(rows_count, send_right)

    def send_left(i):
        pltpu.make_async_remote_copy(
            src_ref=left_sent.at[0],
            dst_ref=left_got.at[my_col],
            send_sem=send_sem.at[1],
            recv_sem=recv_sem.at[1],
            device_id=(my_row, lax.rem(my_col + i + 1, cols_count)),
            device_id_type=MESH,
        ).start()

    each(cols_count - 1, send_left)

    for load in loads[2:]:
        load.wait()
    coupling_row = coupling_own[...]
    near = lax.broadcasted_iota(jnp.int32, (depth, depth), 0) == lax.broadcasted_iota(
        jnp.int32, (depth, depth), 1
    )

    def coefficient(i):
        return jnp.sum(jnp.where(near, coupling_row[i : i + 1], 0.0), axis=1, keepdims=True)

    right_base = coefficient(1) * spread(prev_right_own[...])
    left_base = coefficient(0) * spread(prev_left_own[...])

    def joined(ref, count):
        return jnp.concatenate(
            [sum(ref[i * pack + j] for j in range(pack)) for i in range(count // pack)], axis=1
        )

    arrived(left_got, cols_count - 1, recv_sem.at[1])
    left_rows = joined(left_got, cols_count)
    left_terms = jnp.dot(
        left_rows.astype(jnp.bfloat16), ladder_own[...], preferred_element_type=jnp.float32
    )
    for i in range(rows_count // pack):
        left_part[i] = left_terms[:, i * LANES : (i + 1) * LANES]

    def send_left_part(i):
        slot = lax.rem(my_row + i, rows_count)
        device = my_col * rows_count + slot

        @pl.when(device != me)
        def _():
            pltpu.make_async_remote_copy(
                src_ref=left_part.at[slot // pack],
                dst_ref=left_part_got.at[my_row],
                send_sem=send_sem.at[2],
                recv_sem=recv_sem.at[2],
                device_id=(device // cols_count, lax.rem(device, cols_count)),
                device_id_type=MESH,
            ).start()

    each(rows_count, send_left_part)

    @pl.when(at_home)
    def _():
        left_part_got[pl.ds(my_row, 1)] = left_part[pl.ds(home_slot // pack, 1)]
        arrived(right_got, rows_count - 1, recv_sem.at[0])

    @pl.when(jnp.logical_not(at_home))
    def _():
        arrived(right_got, rows_count, recv_sem.at[0])

    right_cols = joined(right_got, rows_count)
    right_terms = lax.dot_general(
        right_cols.astype(jnp.bfloat16),
        ladder_own[...],
        (((1,), (1,)), ((), ())),
        preferred_element_type=jnp.float32,
    )
    alpha_sent[0] = to_lanes([jnp.sum(left_rows * right_terms, axis=1, keepdims=True)])

    def send_row(src, dst, sems, i):
        pltpu.make_async_remote_copy(
            src_ref=src.at[0],
            dst_ref=dst.at[me],
            send_sem=send_sem.at[sems],
            recv_sem=recv_sem.at[sems],
            device_id=other(i),
            device_id_type=MESH,
        ).start()

    each(devices - 1, functools.partial(send_row, alpha_sent, alpha_got, 4))
    alpha_got[pl.ds(me, 1)] = alpha_sent[...]

    for i in range(cols_count // pack):
        right_part[i] = right_terms[:, i * LANES : (i + 1) * LANES]

    def send_right_part(i):
        col = lax.rem(my_col + i + 1, cols_count)
        pltpu.make_async_remote_copy(
            src_ref=right_part.at[col // pack],
            dst_ref=right_part_got.at[my_col],
            send_sem=send_sem.at[3],
            recv_sem=recv_sem.at[3],
            device_id=(my_row, col),
            device_id_type=MESH,
        ).start()

    each(cols_count - 1, send_right_part)
    right_part_got[pl.ds(my_col, 1)] = right_part[pl.ds(my_col // pack, 1)]

    arrived(right_part_got, cols_count - 1, recv_sem.at[3])
    image_right = jnp.sum(right_part_got[...], axis=0)

    @pl.when(at_home)
    def _():
        arrived(left_part_got, rows_count - 1, recv_sem.at[2])

    @pl.when(jnp.logical_not(at_home))
    def _():
        arrived(left_part_got, rows_count, recv_sem.at[2])

    image_left = jnp.sum(left_part_got[...], axis=0)
    arrived(alpha_got, devices - 1, recv_sem.at[4])
    alpha_row = jnp.sum(alpha_got[...], axis=0) / pairs_total
    alpha_now = to_column(alpha_row, 0)

    right_res = jnp.where(mine, image_right, 0.0) - alpha_now * right - right_base
    left_res = jnp.where(mine, image_left, 0.0) - alpha_now * left - left_base

    norms_sent[0] = to_lanes(
        [
            jnp.sum(left_res * right_res, axis=1, keepdims=True),
            jnp.sum(right_res * right_res, axis=1, keepdims=True),
            jnp.sum(left_res * left_res, axis=1, keepdims=True),
        ]
    )
    each(devices - 1, functools.partial(send_row, norms_sent, norms_got, 5))
    norms_got[pl.ds(me, 1)] = norms_sent[...]

    arrived(right_got, rows_count - 1, send_sem.at[0])
    arrived(left_got, cols_count - 1, send_sem.at[1])
    arrived(left_part_got, rows_count - 1, send_sem.at[2])
    arrived(right_part_got, cols_count - 1, send_sem.at[3])
    arrived(alpha_got, devices - 1, send_sem.at[4])

    @pl.when(jnp.logical_not(at_home))
    def _():
        arrived(right_got, 1, send_sem.at[0])
        arrived(left_part_got, 1, send_sem.at[2])

    arrived(norms_got, devices - 1, recv_sem.at[5])
    norms_row = jnp.sum(norms_got[...], axis=0) / pairs_total
    omega_val = to_column(norms_row, 0)
    right_norm = to_column(norms_row, 1)
    left_norm = to_column(norms_row, 2)
    safe_omega = jnp.maximum(jnp.abs(omega_val), 0.1 * jnp.sqrt(right_norm * left_norm + 1e-06))
    beta_new = jnp.sqrt(safe_omega)
    gamma_new = omega_val / beta_new

    def own_part(array):
        out = array[:, :share]
        for i in range(1, pack):
            out = jnp.where(
                lax.rem(my_col, pack) == i, array[:, i * share : (i + 1) * share], out
            )
        return out

    next_right_out[...] = own_part(right_res / beta_new)
    next_left_out[...] = own_part(left_res * (gamma_new / safe_omega))
    coefficients_out[0:1] = alpha_row[:, :depth]
    coefficients_out[1:2] = to_lanes([beta_new])[:, :depth]
    coefficients_out[2:3] = to_lanes([gamma_new])[:, :depth]
    arrived(norms_got, devices - 1, send_sem.at[5])


def local(rows_count, cols_count, right, left, prev_right, prev_left, coupling, ladder):
    depth, share = right.shape
    devices = rows_count * cols_count
    pack = LANES // share
    f32 = jnp.float32
    vec = pltpu.VMEM((depth, share), f32)

    def tiles(count):
        return pltpu.VMEM((count, depth, LANES), f32)

    return pl.pallas_call(
        functools.partial(kernel, rows_count, cols_count),
        out_shape=(
            jax.ShapeDtypeStruct(right.shape, f32),
            jax.ShapeDtypeStruct(left.shape, f32),
            jax.ShapeDtypeStruct((3, depth), f32),
        ),
        in_specs=[pl.BlockSpec(memory_space=pltpu.HBM)] * 6,
        out_specs=(pl.BlockSpec(memory_space=pltpu.VMEM),) * 3,
        scratch_shapes=[
            vec,
            vec,
            vec,
            vec,
            pltpu.VMEM(coupling.shape, f32),
            pltpu.VMEM(ladder.shape, ladder.dtype),
            tiles(1),
            tiles(1),
            tiles(rows_count),
            tiles(cols_count),
            tiles(cols_count // pack),
            tiles(rows_count // pack),
            tiles(cols_count),
            tiles(rows_count),
            pltpu.VMEM((1, 1, LANES), f32),
            pltpu.VMEM((devices, 1, LANES), f32),
            pltpu.VMEM((1, 1, LANES), f32),
            pltpu.VMEM((devices, 1, LANES), f32),
            pltpu.SemaphoreType.DMA((6,)),
            pltpu.SemaphoreType.DMA((6,)),
            pltpu.SemaphoreType.DMA((6,)),
        ],
        compiler_params=pltpu.CompilerParams(
            collective_id=0, has_side_effects=True, vmem_limit_bytes=32 * 1024 * 1024
        ),
    )(right, left, prev_right, prev_left, coupling, ladder)


def solution(mesh):
    vector = P(None, ("row", "col"))
    return jax.shard_map(
        functools.partial(local, mesh.shape["row"], mesh.shape["col"]),
        mesh=mesh,
        in_specs=(vector, vector, vector, vector, P(), P("row", "col")),
        out_specs=(vector, vector, P()),
        check_vma=False,
    )
```

```python
import functools

import jax
import jax.numpy as jnp
from jax import lax
from jax.experimental import pallas as pl
from jax.experimental.pallas import tpu as pltpu
from jax.sharding import PartitionSpec as P

MESH = pl.DeviceIdType.MESH
LANES = 128
UNROLL_MOST = 32
SMALLEST_SQUARE = 1e-12


def each(count, body):
    if count <= UNROLL_MOST:
        for i in range(count):
            body(i)
    else:
        lax.fori_loop(0, count, lambda i, carry: (body(i), carry)[1], 0)


def arrived(ref, count, sem):
    part = ref.at[pl.ds(0, count)]
    pltpu.make_async_copy(part, part, sem).wait()


def kernel(
    rows_count,
    cols_count,
    right_in,
    left_in,
    prev_right_in,
    prev_left_in,
    coupling_in,
    ladder_in,
    next_right_out,
    next_left_out,
    coefficients_out,
    right_own,
    left_own,
    prev_right_own,
    prev_left_own,
    coupling_own,
    ladder_own,
    right_sent,
    left_sent,
    right_got,
    left_got,
    right_part,
    left_part,
    right_part_got,
    left_part_got,
    sums_sent,
    sums_got,
    load_sem,
    send_sem,
    recv_sem,
):
    devices = rows_count * cols_count
    depth, share = right_own.shape
    pack = LANES // share
    pairs_total = share * devices
    my_row = lax.axis_index("row")
    my_col = lax.axis_index("col")
    me = my_row * cols_count + my_col
    home_col = lax.div(me, rows_count)
    home_slot = lax.rem(me, rows_count)
    at_home = home_col == my_col

    loads = [
        pltpu.make_async_copy(src, dst, load_sem.at[i])
        for i, (src, dst) in enumerate(
            (
                (right_in, right_own),
                (left_in, left_own),
                (prev_right_in, prev_right_own),
                (prev_left_in, prev_left_own),
                (coupling_in, coupling_own),
                (ladder_in, ladder_own),
            )
        )
    ]
    for load in loads:
        load.start()

    def at(device):
        return (lax.div(device, cols_count), lax.rem(device, cols_count))

    def peer(i):
        return (my_row, lax.rem(my_col + i + 1, cols_count))

    def holder(i):
        return at(my_col * rows_count + lax.rem(home_slot + i, rows_count))

    def user(i):
        return (lax.rem(my_row + i, rows_count), home_col)

    def unless_me(i, go):
        if i == 0:
            pl.when(jnp.logical_not(at_home))(go)
        else:
            go()

    barrier = pltpu.get_barrier_semaphore()

    def greet(device):
        pl.semaphore_signal(barrier, inc=1, device_id=device, device_id_type=MESH)

    for i in range(rows_count):
        unless_me(i, lambda: greet(holder(i)))
        unless_me(i, lambda: greet(user(i)))
    for i in range(cols_count - 1):
        greet(peer(i))

    lane = lax.broadcasted_iota(jnp.int32, (depth, LANES), 1)
    sub = lax.broadcasted_iota(jnp.int32, (depth, LANES), 0)
    mine = lane // share == lax.rem(my_col, pack)

    def spread(array):
        return jnp.where(mine, jnp.concatenate([array] * pack, axis=1), 0.0)

    def to_lanes(columns):
        row = jnp.zeros((depth, LANES), jnp.float32)
        for i, column in enumerate(columns):
            row = row + jnp.where(lane == sub + i * depth, column, 0.0)
        return jnp.sum(row, axis=0, keepdims=True)

    def to_column(row, i):
        return jnp.sum(jnp.where(lane == sub + i * depth, row, 0.0), axis=1, keepdims=True)

    loads[0].wait()
    loads[1].wait()
    right = spread(right_own[...])
    left = spread(left_own[...])
    right_sent[0] = right
    left_sent[0] = left
    left_got[pl.ds(my_col, 1)] = left[None]

    @pl.when(at_home)
    def _():
        right_got[pl.ds(home_slot, 1)] = right[None]

    pl.semaphore_wait(barrier, 2 * rows_count + cols_count - 1 - 2 * at_home.astype(jnp.int32))

    def send(src, dst, sems, device):
        pltpu.make_async_remote_copy(
            src_ref=src,
            dst_ref=dst,
            send_sem=send_sem.at[sems],
            recv_sem=recv_sem.at[sems],
            device_id=device,
            device_id_type=MESH,
        ).start()

    for i in (*range(1, rows_count), 0):
        unless_me(i, lambda: send(right_sent.at[0], right_got.at[home_slot], 0, user(i)))
    for i in range(cols_count - 1):
        send(left_sent.at[0], left_got.at[my_col], 1, peer(i))

    for load in loads[2:]:
        load.wait()
    coupling_row = coupling_own[...]
    near = lax.broadcasted_iota(jnp.int32, (depth, depth), 0) == lax.broadcasted_iota(
        jnp.int32, (depth, depth), 1
    )

    def coefficient(i):
        return jnp.sum(jnp.where(near, coupling_row[i : i + 1], 0.0), axis=1, keepdims=True)

    right_base = coefficient(1) * spread(prev_right_own[...])
    left_base = coefficient(0) * spread(prev_left_own[...])

    def joined(ref, count):
        return jnp.concatenate(
            [sum(ref[i * pack + j] for j in range(pack)) for i in range(count // pack)], axis=1
        )

    arrived(left_got, cols_count - 1, recv_sem.at[1])
    left_rows = joined(left_got, cols_count)
    left_terms = jnp.dot(
        left_rows.astype(jnp.bfloat16), ladder_own[...], preferred_element_type=jnp.float32
    )
    for i in range(rows_count // pack):
        left_part[i] = left_terms[:, i * LANES : (i + 1) * LANES]

    for i in (*range(1, rows_count), 0):
        chunk = lax.div(lax.rem(home_slot + i, rows_count), pack)
        unless_me(
            i, lambda: send(left_part.at[chunk], left_part_got.at[my_row], 2, holder(i))
        )

    @pl.when(at_home)
    def _():
        left_part_got[pl.ds(my_row, 1)] = left_part[pl.ds(lax.div(home_slot, pack), 1)]
        arrived(right_got, rows_count - 1, recv_sem.at[0])

    @pl.when(jnp.logical_not(at_home))
    def _():
        arrived(right_got, rows_count, recv_sem.at[0])

    right_cols = joined(right_got, rows_count)
    right_terms = lax.dot_general(
        right_cols.astype(jnp.bfloat16),
        ladder_own[...],
        (((1,), (1,)), ((), ())),
        preferred_element_type=jnp.float32,
    )
    for i in range(cols_count // pack):
        right_part[i] = right_terms[:, i * LANES : (i + 1) * LANES]

    for i in range(cols_count - 1):
        chunk = lax.div(lax.rem(my_col + i + 1, cols_count), pack)
        send(right_part.at[chunk], right_part_got.at[my_col], 3, peer(i))
    right_part_got[pl.ds(my_col, 1)] = right_part[pl.ds(lax.div(my_col, pack), 1)]

    def inner(first, second):
        return jnp.sum(first * second, axis=1, keepdims=True)

    def fitted(product, square):
        usable = square > SMALLEST_SQUARE
        return jnp.where(usable, product / jnp.where(usable, square, 1.0), 0.0)

    right_square = inner(right, right)
    left_square = inner(left, left)
    left_right = inner(left, right)

    arrived(right_part_got, cols_count - 1, recv_sem.at[3])
    image_right = jnp.where(mine, jnp.sum(right_part_got[...], axis=0), 0.0)
    alpha_part = inner(left, image_right)
    right_base = image_right - right_base
    right_fit = fitted(inner(right_base, right), right_square)
    right_rest = right_base - right_fit * right

    @pl.when(at_home)
    def _():
        arrived(left_part_got, rows_count - 1, recv_sem.at[2])

    @pl.when(jnp.logical_not(at_home))
    def _():
        arrived(left_part_got, rows_count, recv_sem.at[2])

    left_base = jnp.where(mine, jnp.sum(left_part_got[...], axis=0), 0.0) - left_base
    left_fit = fitted(inner(left_base, left), left_square)
    left_rest = left_base - left_fit * left

    sums_sent[...] = to_lanes(
        [
            alpha_part,
            right_fit,
            left_fit,
            inner(right_rest, right_rest),
            inner(right_rest, right),
            right_square,
            inner(left_rest, left_rest),
            inner(left_rest, left),
            left_square,
            inner(left_rest, right_rest),
            inner(left_rest, right),
            inner(left, right_rest),
            left_right,
        ]
    )
    each(
        devices - 1,
        lambda i: send(
            sums_sent, sums_got.at[pl.ds(me, 1)], 4, at(lax.rem(me + i + 1, devices))
        ),
    )
    sums_got[pl.ds(me, 1)] = sums_sent[...]

    arrived(right_got, rows_count - 1, send_sem.at[0])
    arrived(left_got, cols_count - 1, send_sem.at[1])
    arrived(left_part_got, rows_count - 1, send_sem.at[2])
    arrived(right_part_got, cols_count - 1, send_sem.at[3])

    @pl.when(jnp.logical_not(at_home))
    def _():
        arrived(right_got, 1, send_sem.at[0])
        arrived(left_part_got, 1, send_sem.at[2])

    arrived(sums_got, devices - 1, recv_sem.at[4])
    sums = sums_got[...]

    def value(i):
        return pltpu.roll(sums, LANES - i * depth, 1)

    def total(values):
        return jnp.sum(values, axis=0, keepdims=True) / pairs_total

    alpha_row = total(sums)
    right_off = value(1) - alpha_row
    left_off = value(2) - alpha_row
    right_norm = to_column(
        total(value(3) + right_off * (2.0 * value(4) + right_off * value(5))), 0
    )
    left_norm = to_column(total(value(6) + left_off * (2.0 * value(7) + left_off * value(8))), 0)
    omega_val = to_column(
        total(
            value(9)
            + right_off * value(10)
            + left_off * value(11)
            + right_off * left_off * value(12)
        ),
        0,
    )
    alpha_now = to_column(alpha_row, 0)
    right_res = right_base - alpha_now * right
    left_res = left_base - alpha_now * left
    safe_omega = jnp.maximum(jnp.abs(omega_val), 0.1 * jnp.sqrt(right_norm * left_norm + 1e-06))
    beta_new = jnp.sqrt(safe_omega)
    gamma_new = omega_val / beta_new

    def own_part(array):
        out = array[:, :share]
        for i in range(1, pack):
            out = jnp.where(
                lax.rem(my_col, pack) == i, array[:, i * share : (i + 1) * share], out
            )
        return out

    next_right_out[...] = own_part(right_res / beta_new)
    next_left_out[...] = own_part(left_res * (gamma_new / safe_omega))
    coefficients_out[0:1] = alpha_row[:, :depth]
    coefficients_out[1:2] = to_lanes([beta_new])[:, :depth]
    coefficients_out[2:3] = to_lanes([gamma_new])[:, :depth]
    arrived(sums_got, devices - 1, send_sem.at[4])


def store(a_in, b_in, c_in, a_out, b_out, c_out, sem):
    copies = [
        pltpu.make_async_copy(src, dst, sem.at[i])
        for i, (src, dst) in enumerate(((a_in, a_out), (b_in, b_out), (c_in, c_out)))
    ]
    for copy in copies:
        copy.start()
    for copy in copies:
        copy.wait()


def local(rows_count, cols_count, right, left, prev_right, prev_left, coupling, ladder):
    depth, share = right.shape
    devices = rows_count * cols_count
    pack = LANES // share
    f32 = jnp.float32
    vec = pltpu.VMEM((depth, share), f32)

    def tiles(count):
        return pltpu.VMEM((count, depth, LANES), f32)

    results = pl.pallas_call(
        functools.partial(kernel, rows_count, cols_count),
        out_shape=(
            jax.ShapeDtypeStruct(right.shape, f32),
            jax.ShapeDtypeStruct(left.shape, f32),
            jax.ShapeDtypeStruct((3, depth), f32),
        ),
        in_specs=[pl.BlockSpec(memory_space=pltpu.HBM)] * 6,
        out_specs=(pl.BlockSpec(memory_space=pltpu.VMEM),) * 3,
        scratch_shapes=[
            vec,
            vec,
            vec,
            vec,
            pltpu.VMEM(coupling.shape, f32),
            pltpu.VMEM(ladder.shape, ladder.dtype),
            tiles(1),
            tiles(1),
            tiles(rows_count),
            tiles(cols_count),
            tiles(cols_count // pack),
            tiles(rows_count // pack),
            tiles(cols_count),
            tiles(rows_count),
            pltpu.VMEM((1, LANES), f32),
            pltpu.VMEM((devices, LANES), f32),
            pltpu.SemaphoreType.DMA((6,)),
            pltpu.SemaphoreType.DMA((5,)),
            pltpu.SemaphoreType.DMA((5,)),
        ],
        compiler_params=pltpu.CompilerParams(
            collective_id=0, has_side_effects=True, vmem_limit_bytes=56 * 1024 * 1024
        ),
    )(right, left, prev_right, prev_left, coupling, ladder)
    return pl.pallas_call(
        store,
        out_shape=tuple(jax.ShapeDtypeStruct(x.shape, x.dtype) for x in results),
        in_specs=[pl.BlockSpec(memory_space=pltpu.HBM)] * 3,
        out_specs=(pl.BlockSpec(memory_space=pltpu.HBM),) * 3,
        scratch_shapes=[pltpu.SemaphoreType.DMA((3,))],
        compiler_params=pltpu.CompilerParams(vmem_limit_bytes=56 * 1024 * 1024),
    )(*results)


def solution(mesh):
    vector = P(None, ("row", "col"))
    return jax.shard_map(
        functools.partial(local, mesh.shape["row"], mesh.shape["col"]),
        mesh=mesh,
        in_specs=(vector, vector, vector, vector, P(), P("row", "col")),
        out_specs=(vector, vector, P()),
        check_vma=False,
    )
```

```python
import functools

import jax
import jax.numpy as jnp
from jax import lax
from jax.experimental import pallas as pl
from jax.experimental.pallas import tpu as pltpu
from jax.sharding import PartitionSpec as P

MESH = pl.DeviceIdType.MESH
LANES = 128
UNROLL_MOST = 32
SMALLEST_SQUARE = 1e-12


def each(count, body):
    if count <= UNROLL_MOST:
        for i in range(count):
            body(i)
    else:
        lax.fori_loop(0, count, lambda i, carry: (body(i), carry)[1], 0)


def arrived(ref, count, sem):
    part = ref.at[pl.ds(0, count)]
    pltpu.make_async_copy(part, part, sem).wait()


def kernel(
    rows_count,
    cols_count,
    right_in,
    left_in,
    prev_right_in,
    prev_left_in,
    coupling_in,
    ladder_in,
    next_right_out,
    next_left_out,
    coefficients_out,
    coupling_own,
    ladder_own,
    right_got,
    left_got,
    mates_got,
    right_part,
    left_part,
    right_part_got,
    left_part_got,
    sums_sent,
    sums_got,
    load_sem,
    send_sem,
    recv_sem,
):
    devices = rows_count * cols_count
    depth, share = right_in.shape
    pack = LANES // share
    pairs_total = share * devices
    my_row = lax.axis_index("row")
    my_col = lax.axis_index("col")
    me = my_row * cols_count + my_col
    home_col = lax.div(me, rows_count)
    home_slot = lax.rem(me, rows_count)
    at_home = home_col == my_col

    groups = devices // pack
    my_group = lax.div(me, pack)
    my_sub = lax.rem(me, pack)
    loads = [
        pltpu.make_async_copy(src, dst, load_sem.at[i])
        for i, (src, dst) in enumerate(
            (
                (left_in, left_got.at[my_col]),
                (ladder_in, ladder_own),
                (coupling_in, coupling_own),
                (right_in, mates_got.at[my_sub, 0]),
                (prev_right_in, mates_got.at[my_sub, 1]),
                (prev_left_in, mates_got.at[my_sub, 2]),
            )
        )
    ]
    home_load = pltpu.make_async_copy(right_in, right_got.at[home_slot], load_sem.at[6])

    def at(device):
        return (lax.div(device, cols_count), lax.rem(device, cols_count))

    def peer(i):
        return (my_row, lax.rem(my_col + i + 1, cols_count))

    def holder(i):
        return at(my_col * rows_count + lax.rem(home_slot + i, rows_count))

    def user(i):
        return (lax.rem(my_row + i, rows_count), home_col)

    def unless_me(i, go):
        if i == 0:
            pl.when(jnp.logical_not(at_home))(go)
        else:
            go()

    barrier = pltpu.get_barrier_semaphore()

    def greet(device):
        pl.semaphore_signal(barrier, inc=1, device_id=device, device_id_type=MESH)

    for i in range(rows_count):
        unless_me(i, lambda: greet(holder(i)))
        unless_me(i, lambda: greet(user(i)))
    for i in range(cols_count - 1):
        greet(peer(i))

    for load in loads:
        load.start()
    pl.when(at_home)(home_load.start)

    lane = lax.broadcasted_iota(jnp.int32, (depth, LANES), 1)
    sub = lax.broadcasted_iota(jnp.int32, (depth, LANES), 0)

    def to_lanes(columns):
        row = jnp.zeros((depth, LANES), jnp.float32)
        for i, column in enumerate(columns):
            row = row + jnp.where(lane == sub + i * depth, column, 0.0)
        return jnp.sum(row, axis=0, keepdims=True)

    def to_column(row, i):
        return jnp.sum(jnp.where(lane == sub + i * depth, row, 0.0), axis=1, keepdims=True)

    pl.semaphore_wait(barrier, 2 * rows_count + cols_count - 1 - 2 * at_home.astype(jnp.int32))

    def send(src, dst, sems, device):
        pltpu.make_async_remote_copy(
            src_ref=src,
            dst_ref=dst,
            send_sem=send_sem.at[sems],
            recv_sem=recv_sem.at[sems],
            device_id=device,
            device_id_type=MESH,
        ).start()

    for i in (*range(1, rows_count), 0):
        unless_me(i, lambda: send(right_in, right_got.at[home_slot], 0, user(i)))
    for i in range(cols_count - 1):
        send(left_in, left_got.at[my_col], 1, peer(i))
    for i in range(pack - 1):
        mate = (my_row, my_col - my_sub + lax.rem(my_sub + i + 1, pack))
        for j, src in enumerate((right_in, prev_right_in, prev_left_in)):
            send(src, mates_got.at[my_sub, j], 5, mate)

    for load in loads:
        load.wait()
    coupling_row = coupling_own[...]
    near = lax.broadcasted_iota(jnp.int32, (depth, depth), 0) == lax.broadcasted_iota(
        jnp.int32, (depth, depth), 1
    )

    def coefficient(i):
        return jnp.sum(jnp.where(near, coupling_row[i : i + 1], 0.0), axis=1, keepdims=True)

    def joined(pieces):
        return jnp.concatenate(pieces, axis=1)

    arrived(left_got, cols_count - 1, recv_sem.at[1])
    left_rows = joined([left_got[i] for i in range(cols_count)])
    left_terms = jnp.dot(
        left_rows.astype(jnp.bfloat16), ladder_own[...], preferred_element_type=jnp.float32
    )
    for i in range(rows_count // pack):
        left_part[i] = left_terms[:, i * LANES : (i + 1) * LANES]

    for i in (*range(1, rows_count), 0):
        chunk = lax.div(lax.rem(home_slot + i, rows_count), pack)
        unless_me(
            i, lambda: send(left_part.at[chunk], left_part_got.at[my_row], 2, holder(i))
        )

    @pl.when(at_home)
    def _():
        home_load.wait()
        left_part_got[pl.ds(my_row, 1)] = left_part[pl.ds(lax.div(home_slot, pack), 1)]
        arrived(right_got, rows_count - 1, recv_sem.at[0])

    @pl.when(jnp.logical_not(at_home))
    def _():
        arrived(right_got, rows_count, recv_sem.at[0])

    right_cols = joined([right_got[i] for i in range(rows_count)])
    right_terms = lax.dot_general(
        right_cols.astype(jnp.bfloat16),
        ladder_own[...],
        (((1,), (1,)), ((), ())),
        preferred_element_type=jnp.float32,
    )
    for i in range(cols_count // pack):
        right_part[i] = right_terms[:, i * LANES : (i + 1) * LANES]

    for i in range(cols_count - 1):
        chunk = lax.div(lax.rem(my_col + i + 1, cols_count), pack)
        send(right_part.at[chunk], right_part_got.at[my_col], 3, peer(i))
    right_part_got[pl.ds(my_col, 1)] = right_part[pl.ds(lax.div(my_col, pack), 1)]

    def inner(first, second):
        return jnp.sum(first * second, axis=1, keepdims=True)

    def fitted(product, square):
        usable = square > SMALLEST_SQUARE
        return jnp.where(usable, product / jnp.where(usable, square, 1.0), 0.0)

    arrived(mates_got, pack - 1, recv_sem.at[5])
    right, prev_right, prev_left = (
        joined([mates_got[i, j] for i in range(pack)]) for j in range(3)
    )
    first_col = my_col - my_sub
    left = joined([left_got[first_col + i] for i in range(pack)])
    right_square = inner(right, right)
    left_square = inner(left, left)
    left_right = inner(left, right)

    arrived(right_part_got, cols_count - 1, recv_sem.at[3])
    image_right = jnp.sum(right_part_got[...], axis=0)
    alpha_part = inner(left, image_right)
    right_base = image_right - coefficient(1) * prev_right
    right_fit = fitted(inner(right_base, right), right_square)
    right_rest = right_base - right_fit * right

    @pl.when(at_home)
    def _():
        arrived(left_part_got, rows_count - 1, recv_sem.at[2])

    @pl.when(jnp.logical_not(at_home))
    def _():
        arrived(left_part_got, rows_count, recv_sem.at[2])

    left_base = jnp.sum(left_part_got[...], axis=0) - coefficient(0) * prev_left
    left_fit = fitted(inner(left_base, left), left_square)
    left_rest = left_base - left_fit * left

    sums_sent[...] = to_lanes(
        [
            alpha_part,
            right_fit,
            left_fit,
            inner(right_rest, right_rest),
            inner(right_rest, right),
            right_square,
            inner(left_rest, left_rest),
            inner(left_rest, left),
            left_square,
            inner(left_rest, right_rest),
            inner(left_rest, right),
            inner(left, right_rest),
            left_right,
        ]
    )
    low = my_group < groups // 2

    def far_first(i):
        down = groups - 1 - i
        down = down - (down <= my_group).astype(jnp.int32)
        up = i + (i >= my_group).astype(jnp.int32)
        return at(jnp.where(low, down, up) * pack + my_sub)

    each(
        groups - 1,
        lambda i: send(sums_sent, sums_got.at[pl.ds(my_group, 1)], 4, far_first(i)),
    )
    sums_got[pl.ds(my_group, 1)] = sums_sent[...]

    arrived(right_got, rows_count - 1, send_sem.at[0])
    arrived(left_got, cols_count - 1, send_sem.at[1])
    arrived(left_part_got, rows_count - 1, send_sem.at[2])
    arrived(right_part_got, cols_count - 1, send_sem.at[3])
    arrived(mates_got, pack - 1, send_sem.at[5])

    @pl.when(jnp.logical_not(at_home))
    def _():
        arrived(right_got, 1, send_sem.at[0])
        arrived(left_part_got, 1, send_sem.at[2])

    arrived(sums_got, groups - 1, recv_sem.at[4])
    sums = sums_got[...]

    def value(i):
        return pltpu.roll(sums, LANES - i * depth, 1)

    def total(values):
        return jnp.sum(values, axis=0, keepdims=True) / pairs_total

    alpha_row = total(sums)
    right_off = value(1) - alpha_row
    left_off = value(2) - alpha_row
    right_norm = to_column(
        total(value(3) + right_off * (2.0 * value(4) + right_off * value(5))), 0
    )
    left_norm = to_column(total(value(6) + left_off * (2.0 * value(7) + left_off * value(8))), 0)
    omega_val = to_column(
        total(
            value(9)
            + right_off * value(10)
            + left_off * value(11)
            + right_off * left_off * value(12)
        ),
        0,
    )
    alpha_now = to_column(alpha_row, 0)
    right_res = right_base - alpha_now * right
    left_res = left_base - alpha_now * left
    safe_omega = jnp.maximum(jnp.abs(omega_val), 0.1 * jnp.sqrt(right_norm * left_norm + 1e-06))
    beta_new = jnp.sqrt(safe_omega)
    gamma_new = omega_val / beta_new

    def own_part(array):
        out = array[:, :share]
        for i in range(1, pack):
            out = jnp.where(
                my_sub == i, array[:, i * share : (i + 1) * share], out
            )
        return out

    next_right_out[...] = own_part(right_res / beta_new)
    next_left_out[...] = own_part(left_res * (gamma_new / safe_omega))
    coefficients_out[0:1] = alpha_row[:, :depth]
    coefficients_out[1:2] = to_lanes([beta_new])[:, :depth]
    coefficients_out[2:3] = to_lanes([gamma_new])[:, :depth]
    arrived(sums_got, groups - 1, send_sem.at[4])


def store(a_in, b_in, c_in, a_out, b_out, c_out, sem):
    copies = [
        pltpu.make_async_copy(src, dst, sem.at[i])
        for i, (src, dst) in enumerate(((a_in, a_out), (b_in, b_out), (c_in, c_out)))
    ]
    for copy in copies:
        copy.start()
    for copy in copies:
        copy.wait()


def local(rows_count, cols_count, right, left, prev_right, prev_left, coupling, ladder):
    depth, share = right.shape
    devices = rows_count * cols_count
    pack = LANES // share
    f32 = jnp.float32

    def tiles(count):
        return pltpu.VMEM((count, depth, LANES), f32)

    results = pl.pallas_call(
        functools.partial(kernel, rows_count, cols_count),
        out_shape=(
            jax.ShapeDtypeStruct(right.shape, f32),
            jax.ShapeDtypeStruct(left.shape, f32),
            jax.ShapeDtypeStruct((3, depth), f32),
        ),
        in_specs=[pl.BlockSpec(memory_space=pltpu.HBM)] * 6,
        out_specs=(pl.BlockSpec(memory_space=pltpu.VMEM),) * 3,
        scratch_shapes=[
            pltpu.VMEM(coupling.shape, f32),
            pltpu.VMEM(ladder.shape, ladder.dtype),
            pltpu.VMEM((rows_count, depth, share), f32),
            pltpu.VMEM((cols_count, depth, share), f32),
            pltpu.VMEM((pack, 3, depth, share), f32),
            tiles(cols_count // pack),
            tiles(rows_count // pack),
            tiles(cols_count),
            tiles(rows_count),
            pltpu.VMEM((1, LANES), f32),
            pltpu.VMEM((devices // pack, LANES), f32),
            pltpu.SemaphoreType.DMA((7,)),
            pltpu.SemaphoreType.DMA((6,)),
            pltpu.SemaphoreType.DMA((6,)),
        ],
        compiler_params=pltpu.CompilerParams(
            collective_id=0, has_side_effects=True, vmem_limit_bytes=56 * 1024 * 1024
        ),
    )(right, left, prev_right, prev_left, coupling, ladder)
    return pl.pallas_call(
        store,
        out_shape=tuple(jax.ShapeDtypeStruct(x.shape, x.dtype) for x in results),
        in_specs=[pl.BlockSpec(memory_space=pltpu.HBM)] * 3,
        out_specs=(pl.BlockSpec(memory_space=pltpu.HBM),) * 3,
        scratch_shapes=[pltpu.SemaphoreType.DMA((3,))],
        compiler_params=pltpu.CompilerParams(vmem_limit_bytes=56 * 1024 * 1024),
    )(*results)


def solution(mesh):
    vector = P(None, ("row", "col"))
    return jax.shard_map(
        functools.partial(local, mesh.shape["row"], mesh.shape["col"]),
        mesh=mesh,
        in_specs=(vector, vector, vector, vector, P(), P("row", "col")),
        out_specs=(vector, vector, P()),
        check_vma=False,
    )
```

```python
import functools

import jax
import jax.numpy as jnp
from jax import lax
from jax.experimental import pallas as pl
from jax.experimental.pallas import tpu as pltpu
from jax.sharding import PartitionSpec as P

MESH = pl.DeviceIdType.MESH
LANES = 128
UNROLL_MOST = 32
SMALLEST_SQUARE = 1e-12


def each(count, body):
    if count <= UNROLL_MOST:
        for i in range(count):
            body(i)
    else:
        lax.fori_loop(0, count, lambda i, carry: (body(i), carry)[1], 0)


def arrived(ref, count, sem):
    part = ref.at[pl.ds(0, count)]
    pltpu.make_async_copy(part, part, sem).wait()


def kernel(
    rows_count,
    cols_count,
    right_in,
    left_in,
    prev_right_in,
    prev_left_in,
    coupling_in,
    ladder_in,
    next_right_out,
    next_left_out,
    coefficients_out,
    coupling_own,
    ladder_own,
    right_got,
    left_got,
    mates_got,
    right_part,
    left_part,
    right_part_got,
    left_part_got,
    sums_sent,
    sums_got,
    load_sem,
    send_sem,
    recv_sem,
):
    devices = rows_count * cols_count
    depth, share = right_in.shape
    pack = LANES // share
    pairs_total = share * devices
    my_row = lax.axis_index("row")
    my_col = lax.axis_index("col")
    me = my_row * cols_count + my_col
    home_col = lax.div(me, rows_count)
    home_slot = lax.rem(me, rows_count)
    at_home = home_col == my_col

    groups = devices // pack
    my_group = lax.div(me, pack)
    my_sub = lax.rem(me, pack)
    loads = [
        pltpu.make_async_copy(src, dst, load_sem.at[i])
        for i, (src, dst) in enumerate(
            (
                (left_in, left_got.at[my_col]),
                (ladder_in, ladder_own),
                (coupling_in, coupling_own),
                (right_in, mates_got.at[my_sub, 0]),
                (prev_right_in, mates_got.at[my_sub, 1]),
                (prev_left_in, mates_got.at[my_sub, 2]),
            )
        )
    ]
    home_load = pltpu.make_async_copy(right_in, right_got.at[home_slot], load_sem.at[6])

    def at(device):
        return (lax.div(device, cols_count), lax.rem(device, cols_count))

    def peer(i):
        return (my_row, lax.rem(my_col + i + 1, cols_count))

    def holder(i):
        return at(my_col * rows_count + lax.rem(home_slot + i, rows_count))

    def user(i):
        return (lax.rem(my_row + i, rows_count), home_col)

    def unless_me(i, go):
        if i == 0:
            pl.when(jnp.logical_not(at_home))(go)
        else:
            go()

    barrier = pltpu.get_barrier_semaphore()

    def greet(device):
        pl.semaphore_signal(barrier, inc=1, device_id=device, device_id_type=MESH)

    for i in range(rows_count):
        unless_me(i, lambda: greet(holder(i)))
        unless_me(i, lambda: greet(user(i)))
    for i in range(cols_count - 1):
        greet(peer(i))

    for load in loads:
        load.start()
    pl.when(at_home)(home_load.start)

    lane = lax.broadcasted_iota(jnp.int32, (depth, LANES), 1)
    sub = lax.broadcasted_iota(jnp.int32, (depth, LANES), 0)

    def to_lanes(columns):
        row = jnp.zeros((depth, LANES), jnp.float32)
        for i, column in enumerate(columns):
            row = row + jnp.where(lane == sub + i * depth, column, 0.0)
        return jnp.sum(row, axis=0, keepdims=True)

    def to_column(row, i):
        return jnp.sum(jnp.where(lane == sub + i * depth, row, 0.0), axis=1, keepdims=True)

    pl.semaphore_wait(barrier, 2 * rows_count + cols_count - 1 - 2 * at_home.astype(jnp.int32))

    def send(src, dst, sems, device):
        pltpu.make_async_remote_copy(
            src_ref=src,
            dst_ref=dst,
            send_sem=send_sem.at[sems],
            recv_sem=recv_sem.at[sems],
            device_id=device,
            device_id_type=MESH,
        ).start()

    for i in (*range(1, rows_count), 0):
        unless_me(i, lambda: send(right_in, right_got.at[home_slot], 0, user(i)))
    for i in range(cols_count - 1):
        send(left_in, left_got.at[my_col], 1, peer(i))
    for i in range(pack - 1):
        mate = (my_row, my_col - my_sub + lax.rem(my_sub + i + 1, pack))
        for j, src in enumerate((right_in, prev_right_in, prev_left_in)):
            send(src, mates_got.at[my_sub, j], 5, mate)

    for load in loads:
        load.wait()
    coupling_row = coupling_own[...]
    near = lax.broadcasted_iota(jnp.int32, (depth, depth), 0) == lax.broadcasted_iota(
        jnp.int32, (depth, depth), 1
    )

    def coefficient(i):
        return jnp.sum(jnp.where(near, coupling_row[i : i + 1], 0.0), axis=1, keepdims=True)

    def joined(pieces):
        return jnp.concatenate(pieces, axis=1)

    arrived(left_got, cols_count - 1, recv_sem.at[1])
    left_rows = joined([left_got[i] for i in range(cols_count)])
    left_terms = jnp.dot(
        left_rows.astype(jnp.bfloat16), ladder_own[...], preferred_element_type=jnp.float32
    )
    for i in range(rows_count // pack):
        left_part[i] = left_terms[:, i * LANES : (i + 1) * LANES]

    for i in (*range(1, rows_count), 0):
        chunk = lax.div(lax.rem(home_slot + i, rows_count), pack)
        unless_me(
            i, lambda: send(left_part.at[chunk], left_part_got.at[my_row], 2, holder(i))
        )

    @pl.when(at_home)
    def _():
        home_load.wait()
        left_part_got[pl.ds(my_row, 1)] = left_part[pl.ds(lax.div(home_slot, pack), 1)]
        arrived(right_got, rows_count - 1, recv_sem.at[0])

    @pl.when(jnp.logical_not(at_home))
    def _():
        arrived(right_got, rows_count, recv_sem.at[0])

    right_cols = joined([right_got[i] for i in range(rows_count)])
    right_terms = lax.dot_general(
        right_cols.astype(jnp.bfloat16),
        ladder_own[...],
        (((1,), (1,)), ((), ())),
        preferred_element_type=jnp.float32,
    )
    for i in range(cols_count // pack):
        right_part[i] = right_terms[:, i * LANES : (i + 1) * LANES]

    for i in range(cols_count - 1):
        chunk = lax.div(lax.rem(my_col + i + 1, cols_count), pack)
        send(right_part.at[chunk], right_part_got.at[my_col], 3, peer(i))
    right_part_got[pl.ds(my_col, 1)] = right_part[pl.ds(lax.div(my_col, pack), 1)]

    def inner(first, second):
        return jnp.sum(first * second, axis=1, keepdims=True)

    def fitted(product, square):
        usable = square > SMALLEST_SQUARE
        return jnp.where(usable, product / jnp.where(usable, square, 1.0), 0.0)

    arrived(mates_got, pack - 1, recv_sem.at[5])
    right, prev_right, prev_left = (
        joined([mates_got[i, j] for i in range(pack)]) for j in range(3)
    )
    first_col = my_col - my_sub
    left = joined([left_got[first_col + i] for i in range(pack)])
    right_square = inner(right, right)
    left_square = inner(left, left)
    left_right = inner(left, right)

    arrived(right_part_got, cols_count - 1, recv_sem.at[3])
    image_right = jnp.sum(right_part_got[...], axis=0)
    alpha_part = inner(left, image_right)
    right_base = image_right - coefficient(1) * prev_right
    right_fit = fitted(inner(right_base, right), right_square)
    right_rest = right_base - right_fit * right

    @pl.when(at_home)
    def _():
        arrived(left_part_got, rows_count - 1, recv_sem.at[2])

    @pl.when(jnp.logical_not(at_home))
    def _():
        arrived(left_part_got, rows_count, recv_sem.at[2])

    left_base = jnp.sum(left_part_got[...], axis=0) - coefficient(0) * prev_left
    left_fit = fitted(inner(left_base, left), left_square)
    left_rest = left_base - left_fit * left

    sums_sent[...] = to_lanes(
        [
            alpha_part,
            right_fit,
            left_fit,
            inner(right_rest, right_rest),
            inner(right_rest, right),
            right_square,
            inner(left_rest, left_rest),
            inner(left_rest, left),
            left_square,
            inner(left_rest, right_rest),
            inner(left_rest, right),
            inner(left, right_rest),
            left_right,
        ]
    )
    low = my_group < groups // 2

    def far_first(i):
        down = groups - 1 - i
        down = down - (down <= my_group).astype(jnp.int32)
        up = i + (i >= my_group).astype(jnp.int32)
        return at(jnp.where(low, down, up) * pack + my_sub)

    each(
        groups - 1,
        lambda i: send(sums_sent, sums_got.at[pl.ds(my_group, 1)], 4, far_first(i)),
    )
    sums_got[pl.ds(my_group, 1)] = sums_sent[...]

    arrived(right_got, rows_count - 1, send_sem.at[0])
    arrived(left_got, cols_count - 1, send_sem.at[1])
    arrived(left_part_got, rows_count - 1, send_sem.at[2])
    arrived(right_part_got, cols_count - 1, send_sem.at[3])
    arrived(mates_got, pack - 1, send_sem.at[5])

    @pl.when(jnp.logical_not(at_home))
    def _():
        arrived(right_got, 1, send_sem.at[0])
        arrived(left_part_got, 1, send_sem.at[2])

    arrived(sums_got, groups - 1, recv_sem.at[4])
    sums = sums_got[...]

    def value(i):
        return pltpu.roll(sums, LANES - i * depth, 1)

    def total(values):
        return jnp.sum(values, axis=0, keepdims=True) / pairs_total

    alpha_row = total(sums)
    right_off = value(1) - alpha_row
    left_off = value(2) - alpha_row
    right_norm = to_column(
        total(value(3) + right_off * (2.0 * value(4) + right_off * value(5))), 0
    )
    left_norm = to_column(total(value(6) + left_off * (2.0 * value(7) + left_off * value(8))), 0)
    omega_val = to_column(
        total(
            value(9)
            + right_off * value(10)
            + left_off * value(11)
            + right_off * left_off * value(12)
        ),
        0,
    )
    alpha_now = to_column(alpha_row, 0)
    right_res = right_base - alpha_now * right
    left_res = left_base - alpha_now * left
    safe_omega = jnp.maximum(jnp.abs(omega_val), 0.1 * jnp.sqrt(right_norm * left_norm + 1e-06))
    beta_new = jnp.sqrt(safe_omega)
    gamma_new = omega_val / beta_new

    def own_part(array):
        out = array[:, :share]
        for i in range(1, pack):
            out = jnp.where(
                my_sub == i, array[:, i * share : (i + 1) * share], out
            )
        return out

    next_right_out[...] = own_part(right_res / beta_new)
    next_left_out[...] = own_part(left_res * (gamma_new / safe_omega))
    coefficients_out[0:1] = alpha_row[:, :depth]
    coefficients_out[1:2] = to_lanes([beta_new])[:, :depth]
    coefficients_out[2:3] = to_lanes([gamma_new])[:, :depth]
    arrived(sums_got, groups - 1, send_sem.at[4])


def store(a_in, b_in, c_in, a_out, b_out, c_out, sem):
    copies = [
        pltpu.make_async_copy(src, dst, sem.at[i])
        for i, (src, dst) in enumerate(((a_in, a_out), (b_in, b_out), (c_in, c_out)))
    ]
    for copy in copies:
        copy.start()
    for copy in copies:
        copy.wait()


def local(rows_count, cols_count, right, left, prev_right, prev_left, coupling, ladder):
    depth, share = right.shape
    devices = rows_count * cols_count
    pack = LANES // share
    f32 = jnp.float32

    def tiles(count):
        return pltpu.VMEM((count, depth, LANES), f32)

    results = pl.pallas_call(
        functools.partial(kernel, rows_count, cols_count),
        out_shape=(
            pltpu.VMEM(right.shape, f32),
            pltpu.VMEM(left.shape, f32),
            pltpu.VMEM((3, depth), f32),
        ),
        in_specs=[pl.BlockSpec(memory_space=pltpu.HBM)] * 6,
        out_specs=(pl.BlockSpec(memory_space=pltpu.VMEM),) * 3,
        scratch_shapes=[
            pltpu.VMEM(coupling.shape, f32),
            pltpu.VMEM(ladder.shape, ladder.dtype),
            pltpu.VMEM((rows_count, depth, share), f32),
            pltpu.VMEM((cols_count, depth, share), f32),
            pltpu.VMEM((pack, 3, depth, share), f32),
            tiles(cols_count // pack),
            tiles(rows_count // pack),
            tiles(cols_count),
            tiles(rows_count),
            pltpu.VMEM((1, LANES), f32),
            pltpu.VMEM((devices // pack, LANES), f32),
            pltpu.SemaphoreType.DMA((7,)),
            pltpu.SemaphoreType.DMA((6,)),
            pltpu.SemaphoreType.DMA((6,)),
        ],
        compiler_params=pltpu.CompilerParams(
            collective_id=0, has_side_effects=True, vmem_limit_bytes=32 * 1024 * 1024
        ),
    )(*(pltpu.with_memory_space_constraint(x, pltpu.HBM) for x in (right, left, prev_right, prev_left, coupling, ladder)))
    return pl.pallas_call(
        store,
        out_shape=tuple(jax.ShapeDtypeStruct(x.shape, x.dtype) for x in results),
        in_specs=[pl.BlockSpec(memory_space=pltpu.VMEM)] * 3,
        out_specs=(pl.BlockSpec(memory_space=pltpu.HBM),) * 3,
        scratch_shapes=[pltpu.SemaphoreType.DMA((3,))],
    )(*results)


def solution(mesh):
    vector = P(None, ("row", "col"))
    return jax.shard_map(
        functools.partial(local, mesh.shape["row"], mesh.shape["col"]),
        mesh=mesh,
        in_specs=(vector, vector, vector, vector, P(), P("row", "col")),
        out_specs=(vector, vector, P()),
        check_vma=False,
    )
```

```python
import functools

import jax
import jax.numpy as jnp
from jax import lax
from jax.experimental import pallas as pl
from jax.experimental.pallas import tpu as pltpu
from jax.sharding import PartitionSpec as P

MESH = pl.DeviceIdType.MESH
LANES = 128
UNROLL_MOST = 32
SMALLEST_SQUARE = 1e-12


def each(count, body):
    if count <= UNROLL_MOST:
        for i in range(count):
            body(i)
    else:
        lax.fori_loop(0, count, lambda i, carry: (body(i), carry)[1], 0)


def arrived(ref, count, sem):
    part = ref.at[pl.ds(0, count)]
    pltpu.make_async_copy(part, part, sem).wait()


def kernel(
    rows_count,
    cols_count,
    right_in,
    left_in,
    prev_right_in,
    prev_left_in,
    coupling_in,
    ladder_in,
    next_right_out,
    next_left_out,
    coefficients_out,
    coupling_own,
    ladder_own,
    right_got,
    left_got,
    mates_got,
    right_part,
    left_part,
    right_part_got,
    left_part_got,
    sums_sent,
    sums_got,
    load_sem,
    send_sem,
    recv_sem,
):
    devices = rows_count * cols_count
    depth, share = right_in.shape
    pack = LANES // share
    pairs_total = share * devices
    my_row = lax.axis_index("row")
    my_col = lax.axis_index("col")
    me = my_row * cols_count + my_col
    home_col = lax.div(me, rows_count)
    home_slot = lax.rem(me, rows_count)
    at_home = home_col == my_col

    groups = devices // pack
    my_group = lax.div(me, pack)
    my_sub = lax.rem(me, pack)
    loads = [
        pltpu.make_async_copy(src, dst, load_sem.at[i])
        for i, (src, dst) in enumerate(
            (
                (left_in, left_got.at[my_col]),
                (ladder_in, ladder_own),
                (coupling_in, coupling_own),
                (right_in, mates_got.at[my_sub, 0]),
                (prev_right_in, mates_got.at[my_sub, 1]),
                (prev_left_in, mates_got.at[my_sub, 2]),
            )
        )
    ]
    home_load = pltpu.make_async_copy(right_in, right_got.at[home_slot], load_sem.at[6])

    def at(device):
        return (lax.div(device, cols_count), lax.rem(device, cols_count))

    def peer(i):
        return (my_row, lax.rem(my_col + i + 1, cols_count))

    def holder(i):
        return at(my_col * rows_count + lax.rem(home_slot + i, rows_count))

    def user(i):
        return (lax.rem(my_row + i, rows_count), home_col)

    def unless_me(i, go):
        if i == 0:
            pl.when(jnp.logical_not(at_home))(go)
        else:
            go()

    barrier = pltpu.get_barrier_semaphore()

    def greet(device):
        pl.semaphore_signal(barrier, inc=1, device_id=device, device_id_type=MESH)

    for i in range(rows_count):
        unless_me(i, lambda: greet(holder(i)))
        unless_me(i, lambda: greet(user(i)))
    for i in range(cols_count - 1):
        greet(peer(i))

    for load in loads:
        load.start()
    pl.when(at_home)(home_load.start)

    lane = lax.broadcasted_iota(jnp.int32, (depth, LANES), 1)
    sub = lax.broadcasted_iota(jnp.int32, (depth, LANES), 0)

    def to_lanes(columns):
        row = jnp.zeros((depth, LANES), jnp.float32)
        for i, column in enumerate(columns):
            row = row + jnp.where(lane == sub + i * depth, column, 0.0)
        return jnp.sum(row, axis=0, keepdims=True)

    def to_column(row, i):
        return jnp.sum(jnp.where(lane == sub + i * depth, row, 0.0), axis=1, keepdims=True)

    pl.semaphore_wait(barrier, 2 * rows_count + cols_count - 1 - 2 * at_home.astype(jnp.int32))

    def send(src, dst, sems, device):
        pltpu.make_async_remote_copy(
            src_ref=src,
            dst_ref=dst,
            send_sem=send_sem.at[sems],
            recv_sem=recv_sem.at[sems],
            device_id=device,
            device_id_type=MESH,
        ).start()

    for i in (*range(1, rows_count), 0):
        unless_me(i, lambda: send(right_in, right_got.at[home_slot], 0, user(i)))
    for i in range(cols_count - 1):
        send(left_in, left_got.at[my_col], 1, peer(i))
    for i in range(pack - 1):
        mate = (my_row, my_col - my_sub + lax.rem(my_sub + i + 1, pack))
        for j, src in enumerate((right_in, prev_right_in, prev_left_in)):
            send(src, mates_got.at[my_sub, j], 5, mate)

    for load in loads:
        load.wait()
    coupling_row = coupling_own[...]
    near = lax.broadcasted_iota(jnp.int32, (depth, depth), 0) == lax.broadcasted_iota(
        jnp.int32, (depth, depth), 1
    )

    def coefficient(i):
        return jnp.sum(jnp.where(near, coupling_row[i : i + 1], 0.0), axis=1, keepdims=True)

    def joined(pieces):
        return jnp.concatenate(pieces, axis=1)

    arrived(left_got, cols_count - 1, recv_sem.at[1])
    left_rows = joined([left_got[i] for i in range(cols_count)])
    left_terms = jnp.dot(
        left_rows.astype(jnp.bfloat16), ladder_own[...], preferred_element_type=jnp.float32
    )
    for i in range(rows_count // pack):
        left_part[i] = left_terms[:, i * LANES : (i + 1) * LANES]

    for i in (*range(1, rows_count), 0):
        chunk = lax.div(lax.rem(home_slot + i, rows_count), pack)
        unless_me(
            i, lambda: send(left_part.at[chunk], left_part_got.at[my_row], 2, holder(i))
        )

    @pl.when(at_home)
    def _():
        home_load.wait()
        left_part_got[pl.ds(my_row, 1)] = left_part[pl.ds(lax.div(home_slot, pack), 1)]
        arrived(right_got, rows_count - 1, recv_sem.at[0])

    @pl.when(jnp.logical_not(at_home))
    def _():
        arrived(right_got, rows_count, recv_sem.at[0])

    right_cols = joined([right_got[i] for i in range(rows_count)])
    right_terms = lax.dot_general(
        right_cols.astype(jnp.bfloat16),
        ladder_own[...],
        (((1,), (1,)), ((), ())),
        preferred_element_type=jnp.float32,
    )
    for i in range(cols_count // pack):
        right_part[i] = right_terms[:, i * LANES : (i + 1) * LANES]

    for i in range(cols_count - 1):
        chunk = lax.div(lax.rem(my_col + i + 1, cols_count), pack)
        send(right_part.at[chunk], right_part_got.at[my_col], 3, peer(i))
    right_part_got[pl.ds(my_col, 1)] = right_part[pl.ds(lax.div(my_col, pack), 1)]

    def inner(first, second):
        return jnp.sum(first * second, axis=1, keepdims=True)

    def fitted(product, square):
        usable = square > SMALLEST_SQUARE
        return jnp.where(usable, product / jnp.where(usable, square, 1.0), 0.0)

    arrived(mates_got, pack - 1, recv_sem.at[5])
    right, prev_right, prev_left = (
        joined([mates_got[i, j] for i in range(pack)]) for j in range(3)
    )
    first_col = my_col - my_sub
    left = joined([left_got[first_col + i] for i in range(pack)])
    right_square = inner(right, right)
    left_square = inner(left, left)
    left_right = inner(left, right)

    arrived(right_part_got, cols_count - 1, recv_sem.at[3])
    image_right = jnp.sum(right_part_got[...], axis=0)
    alpha_part = inner(left, image_right)
    right_base = image_right - coefficient(1) * prev_right
    right_fit = fitted(inner(right_base, right), right_square)
    right_rest = right_base - right_fit * right

    @pl.when(at_home)
    def _():
        arrived(left_part_got, rows_count - 1, recv_sem.at[2])

    @pl.when(jnp.logical_not(at_home))
    def _():
        arrived(left_part_got, rows_count, recv_sem.at[2])

    left_base = jnp.sum(left_part_got[...], axis=0) - coefficient(0) * prev_left
    left_fit = fitted(inner(left_base, left), left_square)
    left_rest = left_base - left_fit * left

    sums_sent[...] = to_lanes(
        [
            alpha_part,
            right_fit,
            left_fit,
            inner(right_rest, right_rest),
            inner(right_rest, right),
            right_square,
            inner(left_rest, left_rest),
            inner(left_rest, left),
            left_square,
            inner(left_rest, right_rest),
            inner(left_rest, right),
            inner(left, right_rest),
            left_right,
        ]
    )
    low = my_group < groups // 2

    def far_first(i):
        down = groups - 1 - i
        down = down - (down <= my_group).astype(jnp.int32)
        up = i + (i >= my_group).astype(jnp.int32)
        return at(jnp.where(low, down, up) * pack + my_sub)

    each(
        groups - 1,
        lambda i: send(sums_sent, sums_got.at[pl.ds(my_group, 1)], 4, far_first(i)),
    )
    sums_got[pl.ds(my_group, 1)] = sums_sent[...]

    arrived(right_got, rows_count - 1, send_sem.at[0])
    arrived(left_got, cols_count - 1, send_sem.at[1])
    arrived(left_part_got, rows_count - 1, send_sem.at[2])
    arrived(right_part_got, cols_count - 1, send_sem.at[3])
    arrived(mates_got, pack - 1, send_sem.at[5])

    @pl.when(jnp.logical_not(at_home))
    def _():
        arrived(right_got, 1, send_sem.at[0])
        arrived(left_part_got, 1, send_sem.at[2])

    arrived(sums_got, groups - 1, recv_sem.at[4])
    sums = sums_got[...]

    def value(i):
        return pltpu.roll(sums, LANES - i * depth, 1)

    def total(values):
        return jnp.sum(values, axis=0, keepdims=True) / pairs_total

    alpha_row = total(sums)
    right_off = value(1) - alpha_row
    left_off = value(2) - alpha_row
    right_norm = to_column(
        total(value(3) + right_off * (2.0 * value(4) + right_off * value(5))), 0
    )
    left_norm = to_column(total(value(6) + left_off * (2.0 * value(7) + left_off * value(8))), 0)
    omega_val = to_column(
        total(
            value(9)
            + right_off * value(10)
            + left_off * value(11)
            + right_off * left_off * value(12)
        ),
        0,
    )
    alpha_now = to_column(alpha_row, 0)
    right_res = right_base - alpha_now * right
    left_res = left_base - alpha_now * left
    safe_omega = jnp.maximum(jnp.abs(omega_val), 0.1 * jnp.sqrt(right_norm * left_norm + 1e-06))
    beta_new = jnp.sqrt(safe_omega)
    gamma_new = omega_val / beta_new

    def own_part(array):
        out = array[:, :share]
        for i in range(1, pack):
            out = jnp.where(
                my_sub == i, array[:, i * share : (i + 1) * share], out
            )
        return out

    next_right_out[...] = own_part(right_res / beta_new)
    next_left_out[...] = own_part(left_res * (gamma_new / safe_omega))
    coefficients_out[0:1] = alpha_row[:, :depth]
    coefficients_out[1:2] = to_lanes([beta_new])[:, :depth]
    coefficients_out[2:3] = to_lanes([gamma_new])[:, :depth]
    arrived(sums_got, groups - 1, send_sem.at[4])


def store(a_in, b_in, c_in, a_out, b_out, c_out, sem):
    copies = [
        pltpu.make_async_copy(src, dst, sem.at[i])
        for i, (src, dst) in enumerate(((a_in, a_out), (b_in, b_out), (c_in, c_out)))
    ]
    for copy in copies:
        copy.start()
    for copy in copies:
        copy.wait()


def local(rows_count, cols_count, right, left, prev_right, prev_left, coupling, ladder):
    depth, share = right.shape
    devices = rows_count * cols_count
    pack = LANES // share
    f32 = jnp.float32

    def tiles(count):
        return pltpu.VMEM((count, depth, LANES), f32)

    results = pl.pallas_call(
        functools.partial(kernel, rows_count, cols_count),
        out_shape=(
            pltpu.VMEM(right.shape, f32),
            pltpu.VMEM(left.shape, f32),
            pltpu.VMEM((3, depth), f32),
        ),
        in_specs=[pl.BlockSpec(memory_space=pltpu.HBM)] * 6,
        out_specs=(pl.BlockSpec(memory_space=pltpu.VMEM),) * 3,
        scratch_shapes=[
            pltpu.VMEM(coupling.shape, f32),
            pltpu.VMEM(ladder.shape, ladder.dtype),
            pltpu.VMEM((rows_count, depth, share), f32),
            pltpu.VMEM((cols_count, depth, share), f32),
            pltpu.VMEM((pack, 3, depth, share), f32),
            tiles(cols_count // pack),
            tiles(rows_count // pack),
            tiles(cols_count),
            tiles(rows_count),
            pltpu.VMEM((1, LANES), f32),
            pltpu.VMEM((devices // pack, LANES), f32),
            pltpu.SemaphoreType.DMA((7,)),
            pltpu.SemaphoreType.DMA((6,)),
            pltpu.SemaphoreType.DMA((6,)),
        ],
        compiler_params=pltpu.CompilerParams(
            collective_id=0, has_side_effects=True, vmem_limit_bytes=32 * 1024 * 1024
        ),
    )(*(pltpu.with_memory_space_constraint(x, pltpu.HBM) for x in (right, left, prev_right, prev_left, coupling, ladder)))
    return pl.pallas_call(
        store,
        out_shape=tuple(jax.ShapeDtypeStruct(x.shape, x.dtype) for x in results),
        in_specs=[pl.BlockSpec(memory_space=pltpu.VMEM)] * 3,
        out_specs=(pl.BlockSpec(memory_space=pltpu.HBM),) * 3,
        scratch_shapes=[pltpu.SemaphoreType.DMA((3,))],
        compiler_params=pltpu.CompilerParams(vmem_limit_bytes=1024 * 1024),
    )(*(pltpu.with_memory_space_constraint(x, pltpu.VMEM) for x in results))


def solution(mesh):
    vector = P(None, ("row", "col"))
    return jax.shard_map(
        functools.partial(local, mesh.shape["row"], mesh.shape["col"]),
        mesh=mesh,
        in_specs=(vector, vector, vector, vector, P(), P("row", "col")),
        out_specs=(vector, vector, P()),
        check_vma=False,
    )
```

```python
import functools

import jax
import jax.numpy as jnp
from jax import lax
from jax.experimental import pallas as pl
from jax.experimental.pallas import tpu as pltpu
from jax.sharding import PartitionSpec as P

MESH = pl.DeviceIdType.MESH
LANES = 128
LAYERS = 4
UNROLL_MOST = 32
SMALLEST_SQUARE = 1e-12


def each(count, body):
    if count <= UNROLL_MOST:
        for i in range(count):
            body(i)
    else:
        lax.fori_loop(0, count, lambda i, carry: (body(i), carry)[1], 0)


def arrived(ref, count, sem):
    part = ref.at[pl.ds(0, count)]
    pltpu.make_async_copy(part, part, sem).wait()


def kernel(
    rows_count,
    cols_count,
    right_in,
    left_in,
    prev_right_in,
    prev_left_in,
    coupling_in,
    ladder_in,
    next_right_out,
    next_left_out,
    coefficients_out,
    coupling_own,
    ladder_own,
    right_got,
    left_got,
    mates_got,
    chain_got,
    right_block,
    left_sum,
    right_part,
    left_part,
    right_part_got,
    left_part_got,
    sums_sent,
    sums_got,
    load_sem,
    send_sem,
    recv_sem,
):
    devices = rows_count * cols_count
    depth, share = right_in.shape
    pack = LANES // share
    pairs_total = share * devices
    my_row = lax.axis_index("row")
    my_col = lax.axis_index("col")
    me = my_row * cols_count + my_col
    home_col = lax.div(me, rows_count)
    home_slot = lax.rem(me, rows_count)
    at_home = home_col == my_col

    layers = LAYERS if rows_count % LAYERS == 0 else 1
    span = rows_count // layers
    layer = lax.div(my_row, span)
    source_layer = lax.div(lax.div(my_col * rows_count, cols_count), span)
    above = layer > source_layer
    below = layer < source_layer
    highest = layer == layers - 1
    first_row = source_layer * span

    groups = devices // pack
    my_group = lax.div(me, pack)
    my_sub = lax.rem(me, pack)
    loads = [
        pltpu.make_async_copy(src, dst, load_sem.at[i])
        for i, (src, dst) in enumerate(
            (
                (left_in, left_got.at[my_col]),
                (ladder_in, ladder_own),
                (coupling_in, coupling_own),
                (right_in, mates_got.at[my_sub, 0]),
                (prev_right_in, mates_got.at[my_sub, 1]),
                (prev_left_in, mates_got.at[my_sub, 2]),
            )
        )
    ]
    home_load = pltpu.make_async_copy(right_in, right_got.at[home_slot], load_sem.at[6])

    def at(device):
        return (lax.div(device, cols_count), lax.rem(device, cols_count))

    def peer(i):
        return (my_row, lax.rem(my_col + i + 1, cols_count))

    def holder(i):
        return at(my_col * rows_count + lax.rem(home_slot + i, rows_count))

    def unless_me(i, go):
        if i == 0:
            pl.when(jnp.logical_not(at_home))(go)
        else:
            go()

    barrier = pltpu.get_barrier_semaphore()

    def greet(device):
        pl.semaphore_signal(barrier, inc=1, device_id=device, device_id_type=MESH)

    def not_me(row):
        return jnp.logical_not(jnp.logical_and(at_home, my_row == row))

    def by_place(go):
        for place in range(layers):
            for home in (0, 1):
                here = jnp.logical_and(layer == place, at_home == bool(home))
                pl.when(here)(functools.partial(go, place, home))

    for i in range(cols_count - 1):
        greet(peer(i))

    @pl.when(layer > 0)
    def _():
        greet((my_row - span, my_col))

    @pl.when(jnp.logical_not(above))
    def _():
        for i in range(rows_count):
            unless_me(i, lambda: greet(holder(i)))

    for row in range(rows_count):
        pl.when(jnp.logical_and(row >= layer * span, not_me(row)))(
            functools.partial(greet, (row, home_col))
        )

    for load in loads:
        load.start()
    pl.when(at_home)(home_load.start)

    lane = lax.broadcasted_iota(jnp.int32, (depth, LANES), 1)
    sub = lax.broadcasted_iota(jnp.int32, (depth, LANES), 0)

    def to_lanes(columns):
        row = jnp.zeros((depth, LANES), jnp.float32)
        for i, column in enumerate(columns):
            row = row + jnp.where(lane == sub + i * depth, column, 0.0)
        return jnp.sum(row, axis=0, keepdims=True)

    def to_column(row, i):
        return jnp.sum(jnp.where(lane == sub + i * depth, row, 0.0), axis=1, keepdims=True)

    own = at_home.astype(jnp.int32)
    awaited = cols_count - 1 + (layer + 1) * span - own
    awaited = awaited + jnp.where(below, 0, rows_count - own) + jnp.where(highest, 0, 1)
    pl.semaphore_wait(barrier, awaited)

    def send(src, dst, sems, device):
        pltpu.make_async_remote_copy(
            src_ref=src,
            dst_ref=dst,
            send_sem=send_sem.at[sems],
            recv_sem=recv_sem.at[sems],
            device_id=device,
            device_id_type=MESH,
        ).start()

    def send_up(src):
        send(src, chain_got, 6, (my_row + span, my_col))

    for i in range(cols_count - 1):
        send(left_in, left_got.at[my_col], 1, peer(i))
    for row in range(rows_count):
        pl.when(jnp.logical_and(row < (layer + 1) * span, not_me(row)))(
            functools.partial(send, right_in, right_got.at[home_slot], 0, (row, home_col))
        )
    for i in range(pack - 1):
        mate = (my_row, my_col - my_sub + lax.rem(my_sub + i + 1, pack))
        for j, src in enumerate((right_in, prev_right_in, prev_left_in)):
            send(src, mates_got.at[my_sub, j], 5, mate)

    for load in loads:
        load.wait()
    coupling_row = coupling_own[...]
    near = lax.broadcasted_iota(jnp.int32, (depth, depth), 0) == lax.broadcasted_iota(
        jnp.int32, (depth, depth), 1
    )

    def coefficient(i):
        return jnp.sum(jnp.where(near, coupling_row[i : i + 1], 0.0), axis=1, keepdims=True)

    def joined(pieces):
        return jnp.concatenate(pieces, axis=1)

    arrived(left_got, cols_count - 1, recv_sem.at[1])
    left_rows = joined([left_got[i] for i in range(cols_count)])
    left_terms = jnp.dot(
        left_rows.astype(jnp.bfloat16), ladder_own[...], preferred_element_type=jnp.float32
    )
    for i in range(rows_count // pack):
        left_part[i] = left_terms[:, i * LANES : (i + 1) * LANES]

    @pl.when(jnp.logical_and(layer > 0, jnp.logical_not(above)))
    def _():
        arrived(chain_got, rows_count // pack, recv_sem.at[6])
        left_part[...] += chain_got[...]

    @pl.when(below)
    def _():
        send_up(left_part)

    @pl.when(jnp.logical_not(below))
    def _():
        for i in (*range(1, rows_count), 0):
            chunk = lax.div(lax.rem(home_slot + i, rows_count), pack)
            unless_me(
                i,
                lambda: send(
                    left_part.at[chunk], left_part_got.at[my_row - first_row], 2, holder(i)
                ),
            )

    @pl.when(at_home)
    def _():
        home_load.wait()
        left_part_got[pl.ds(my_row - first_row, 1)] = left_part[
            pl.ds(lax.div(home_slot, pack), 1)
        ]
        arrived(right_got, rows_count - 1, recv_sem.at[0])

    @pl.when(jnp.logical_not(jnp.logical_or(at_home, above)))
    def _():
        arrived(right_got, rows_count, recv_sem.at[0])

    @pl.when(jnp.logical_not(above))
    def _():
        for i in range(rows_count // pack):
            right_block[i] = joined([right_got[i * pack + j] for j in range(pack)])

        @pl.when(jnp.logical_not(jnp.logical_or(below, highest)))
        def _():
            send_up(right_block)

    @pl.when(above)
    def _():
        arrived(chain_got, rows_count // pack, recv_sem.at[6])

        @pl.when(jnp.logical_not(highest))
        def _():
            send_up(chain_got)

        right_block[...] = chain_got[...]

    right_cols = joined([right_block[i] for i in range(rows_count // pack)])
    right_terms = lax.dot_general(
        right_cols.astype(jnp.bfloat16),
        ladder_own[...],
        (((1,), (1,)), ((), ())),
        preferred_element_type=jnp.float32,
    )
    for i in range(cols_count // pack):
        right_part[i] = right_terms[:, i * LANES : (i + 1) * LANES]

    for i in range(cols_count - 1):
        chunk = lax.div(lax.rem(my_col + i + 1, cols_count), pack)
        send(right_part.at[chunk], right_part_got.at[my_col], 3, peer(i))
    right_part_got[pl.ds(my_col, 1)] = right_part[pl.ds(lax.div(my_col, pack), 1)]

    def inner(first, second):
        return jnp.sum(first * second, axis=1, keepdims=True)

    def fitted(product, square):
        usable = square > SMALLEST_SQUARE
        return jnp.where(usable, product / jnp.where(usable, square, 1.0), 0.0)

    arrived(mates_got, pack - 1, recv_sem.at[5])
    right, prev_right, prev_left = (
        joined([mates_got[i, j] for i in range(pack)]) for j in range(3)
    )
    first_col = my_col - my_sub
    left = joined([left_got[first_col + i] for i in range(pack)])
    right_square = inner(right, right)
    left_square = inner(left, left)
    left_right = inner(left, right)

    arrived(right_part_got, cols_count - 1, recv_sem.at[3])
    image_right = jnp.sum(right_part_got[...], axis=0)
    alpha_part = inner(left, image_right)
    right_base = image_right - coefficient(1) * prev_right
    right_fit = fitted(inner(right_base, right), right_square)
    right_rest = right_base - right_fit * right

    def add_left(place, home):
        count = (layers - place) * span
        arrived(left_part_got, count - home, recv_sem.at[2])
        left_sum[...] = jnp.sum(left_part_got[0:count], axis=0)

    by_place(add_left)
    left_base = left_sum[...] - coefficient(0) * prev_left
    left_fit = fitted(inner(left_base, left), left_square)
    left_rest = left_base - left_fit * left

    sums_sent[...] = to_lanes(
        [
            alpha_part,
            right_fit,
            left_fit,
            inner(right_rest, right_rest),
            inner(right_rest, right),
            right_square,
            inner(left_rest, left_rest),
            inner(left_rest, left),
            left_square,
            inner(left_rest, right_rest),
            inner(left_rest, right),
            inner(left, right_rest),
            left_right,
        ]
    )
    low = my_group < groups // 2

    def far_first(i):
        down = groups - 1 - i
        down = down - (down <= my_group).astype(jnp.int32)
        up = i + (i >= my_group).astype(jnp.int32)
        return at(jnp.where(low, down, up) * pack + my_sub)

    each(
        groups - 1,
        lambda i: send(sums_sent, sums_got.at[pl.ds(my_group, 1)], 4, far_first(i)),
    )
    sums_got[pl.ds(my_group, 1)] = sums_sent[...]

    arrived(left_got, cols_count - 1, send_sem.at[1])
    arrived(right_part_got, cols_count - 1, send_sem.at[3])
    arrived(mates_got, pack - 1, send_sem.at[5])
    by_place(
        lambda place, home: arrived(right_got, (place + 1) * span - home, send_sem.at[0])
    )

    @pl.when(at_home)
    def _():
        arrived(left_part_got, rows_count - 1, send_sem.at[2])

    @pl.when(jnp.logical_not(jnp.logical_or(at_home, below)))
    def _():
        arrived(left_part_got, rows_count, send_sem.at[2])

    @pl.when(jnp.logical_not(highest))
    def _():
        arrived(chain_got, rows_count // pack, send_sem.at[6])

    arrived(sums_got, groups - 1, recv_sem.at[4])
    sums = sums_got[...]

    def value(i):
        return pltpu.roll(sums, LANES - i * depth, 1)

    def total(values):
        return jnp.sum(values, axis=0, keepdims=True) / pairs_total

    alpha_row = total(sums)
    right_off = value(1) - alpha_row
    left_off = value(2) - alpha_row
    right_norm = to_column(
        total(value(3) + right_off * (2.0 * value(4) + right_off * value(5))), 0
    )
    left_norm = to_column(total(value(6) + left_off * (2.0 * value(7) + left_off * value(8))), 0)
    omega_val = to_column(
        total(
            value(9)
            + right_off * value(10)
            + left_off * value(11)
            + right_off * left_off * value(12)
        ),
        0,
    )
    alpha_now = to_column(alpha_row, 0)
    right_res = right_base - alpha_now * right
    left_res = left_base - alpha_now * left
    safe_omega = jnp.maximum(jnp.abs(omega_val), 0.1 * jnp.sqrt(right_norm * left_norm + 1e-06))
    beta_new = jnp.sqrt(safe_omega)
    gamma_new = omega_val / beta_new

    def own_part(array):
        out = array[:, :share]
        for i in range(1, pack):
            out = jnp.where(
                my_sub == i, array[:, i * share : (i + 1) * share], out
            )
        return out

    next_right_out[...] = own_part(right_res / beta_new)
    next_left_out[...] = own_part(left_res * (gamma_new / safe_omega))
    coefficients_out[0:1] = alpha_row[:, :depth]
    coefficients_out[1:2] = to_lanes([beta_new])[:, :depth]
    coefficients_out[2:3] = to_lanes([gamma_new])[:, :depth]
    arrived(sums_got, groups - 1, send_sem.at[4])


def store(a_in, b_in, c_in, a_out, b_out, c_out, sem):
    copies = [
        pltpu.make_async_copy(src, dst, sem.at[i])
        for i, (src, dst) in enumerate(((a_in, a_out), (b_in, b_out), (c_in, c_out)))
    ]
    for copy in copies:
        copy.start()
    for copy in copies:
        copy.wait()


def local(rows_count, cols_count, right, left, prev_right, prev_left, coupling, ladder):
    depth, share = right.shape
    devices = rows_count * cols_count
    pack = LANES // share
    f32 = jnp.float32

    def tiles(count):
        return pltpu.VMEM((count, depth, LANES), f32)

    results = pl.pallas_call(
        functools.partial(kernel, rows_count, cols_count),
        out_shape=(
            pltpu.VMEM(right.shape, f32),
            pltpu.VMEM(left.shape, f32),
            pltpu.VMEM((3, depth), f32),
        ),
        in_specs=[pl.BlockSpec(memory_space=pltpu.HBM)] * 6,
        out_specs=(pl.BlockSpec(memory_space=pltpu.VMEM),) * 3,
        scratch_shapes=[
            pltpu.VMEM(coupling.shape, f32),
            pltpu.VMEM(ladder.shape, ladder.dtype),
            pltpu.VMEM((rows_count, depth, share), f32),
            pltpu.VMEM((cols_count, depth, share), f32),
            pltpu.VMEM((pack, 3, depth, share), f32),
            tiles(rows_count // pack),
            tiles(rows_count // pack),
            pltpu.VMEM((depth, LANES), f32),
            tiles(cols_count // pack),
            tiles(rows_count // pack),
            tiles(cols_count),
            tiles(rows_count),
            pltpu.VMEM((1, LANES), f32),
            pltpu.VMEM((devices // pack, LANES), f32),
            pltpu.SemaphoreType.DMA((7,)),
            pltpu.SemaphoreType.DMA((7,)),
            pltpu.SemaphoreType.DMA((7,)),
        ],
        compiler_params=pltpu.CompilerParams(
            collective_id=0, has_side_effects=True, vmem_limit_bytes=32 * 1024 * 1024
        ),
    )(*(pltpu.with_memory_space_constraint(x, pltpu.HBM) for x in (right, left, prev_right, prev_left, coupling, ladder)))
    return pl.pallas_call(
        store,
        out_shape=tuple(jax.ShapeDtypeStruct(x.shape, x.dtype) for x in results),
        in_specs=[pl.BlockSpec(memory_space=pltpu.VMEM)] * 3,
        out_specs=(pl.BlockSpec(memory_space=pltpu.HBM),) * 3,
        scratch_shapes=[pltpu.SemaphoreType.DMA((3,))],
        compiler_params=pltpu.CompilerParams(vmem_limit_bytes=1024 * 1024),
    )(*(pltpu.with_memory_space_constraint(x, pltpu.VMEM) for x in results))


def solution(mesh):
    vector = P(None, ("row", "col"))
    return jax.shard_map(
        functools.partial(local, mesh.shape["row"], mesh.shape["col"]),
        mesh=mesh,
        in_specs=(vector, vector, vector, vector, P(), P("row", "col")),
        out_specs=(vector, vector, P()),
        check_vma=False,
    )
```

```python
import functools

import jax
import jax.numpy as jnp
from jax import lax
from jax.experimental import pallas as pl
from jax.experimental.pallas import tpu as pltpu
from jax.sharding import PartitionSpec as P

LOGICAL = pl.DeviceIdType.LOGICAL
LANES = 128
UNROLL_MOST = 32
SMALLEST_SQUARE = 1e-12


def each(count, body):
    if count <= UNROLL_MOST:
        for i in range(count):
            body(i)
    else:
        lax.fori_loop(0, count, lambda i, carry: (body(i), carry)[1], 0)


def arrived(ref, count, sem):
    part = ref.at[pl.ds(0, count)]
    pltpu.make_async_copy(part, part, sem).wait()


def kernel(
    rows_count,
    cols_count,
    right_in,
    left_in,
    prev_right_in,
    prev_left_in,
    coupling_in,
    ladder_in,
    next_right_out,
    next_left_out,
    coefficients_out,
    vectors_own,
    coupling_own,
    ladder_own,
    left_sent,
    mates_sent,
    right_got,
    left_got,
    mates_got,
    right_part,
    left_part,
    right_part_got,
    left_part_got,
    sums_sent,
    sums_got,
    load_sem,
    send_sem,
    recv_sem,
):
    devices = rows_count * cols_count
    depth, share = right_in.shape
    pack = LANES // share
    pairs_total = share * devices
    my_row = lax.axis_index("row")
    my_col = lax.axis_index("col")
    me = my_row * cols_count + my_col
    home_col = lax.div(me, rows_count)
    home_slot = lax.rem(me, rows_count)
    at_home = home_col == my_col

    groups = devices // pack
    my_group = lax.div(me, pack)
    my_sub = lax.rem(me, pack)
    loads = [
        pltpu.make_async_copy(src, dst, load_sem.at[i])
        for i, (src, dst) in enumerate(
            (
                (right_in, vectors_own.at[0]),
                (left_in, vectors_own.at[1]),
                (prev_right_in, vectors_own.at[2]),
                (prev_left_in, vectors_own.at[3]),
                (coupling_in, coupling_own),
                (ladder_in, ladder_own),
            )
        )
    ]
    row_start = my_row * cols_count

    def peer(i):
        return row_start + lax.rem(my_col + i + 1, cols_count)

    def holder(i):
        return my_col * rows_count + lax.rem(home_slot + i, rows_count)

    def user(i):
        return lax.rem(my_row + i, rows_count) * cols_count + home_col

    def unless_me(i, go):
        if i == 0:
            pl.when(jnp.logical_not(at_home))(go)
        else:
            go()

    barrier = pltpu.get_barrier_semaphore()

    def greet(device):
        pl.semaphore_signal(barrier, inc=1, device_id=device, device_id_type=LOGICAL)

    for i in range(cols_count - 1):
        greet(peer(i))
    for load in loads[:2]:
        load.start()
    for i in range(rows_count):
        unless_me(i, lambda: greet(holder(i)))
    for i in range(rows_count):
        unless_me(i, lambda: greet(user(i)))
    for load in loads[2:]:
        load.start()

    lane = lax.broadcasted_iota(jnp.int32, (depth, LANES), 1)
    sub = lax.broadcasted_iota(jnp.int32, (depth, LANES), 0)

    mine = lane // share == my_sub

    def spread(i):
        return jnp.where(mine, jnp.concatenate([vectors_own[i]] * pack, axis=1), 0.0)

    def to_lanes(columns):
        row = jnp.zeros((depth, LANES), jnp.float32)
        for i, column in enumerate(columns):
            row = row + jnp.where(lane == sub + i * depth, column, 0.0)
        return jnp.sum(row, axis=0, keepdims=True)

    def to_column(row, i):
        return jnp.sum(jnp.where(lane == sub + i * depth, row, 0.0), axis=1, keepdims=True)

    for load in loads[:2]:
        load.wait()
    right_own = spread(0)
    left_own = spread(1)
    mates_sent[0] = right_own
    left_sent[0] = left_own
    left_got[pl.ds(my_col, 1)] = left_own[None]

    @pl.when(at_home)
    def _():
        right_got[pl.ds(home_slot, 1)] = right_own[None]

    pl.semaphore_wait(barrier, 2 * rows_count + cols_count - 1 - 2 * at_home.astype(jnp.int32))

    def send(src, dst, sems, device):
        pltpu.make_async_remote_copy(
            src_ref=src,
            dst_ref=dst,
            send_sem=send_sem.at[sems],
            recv_sem=recv_sem.at[sems],
            device_id=device,
            device_id_type=LOGICAL,
        ).start()

    for i in range(cols_count - 1):
        send(left_sent.at[0], left_got.at[my_col], 1, peer(i))
    for i in (*range(1, rows_count), 0):
        unless_me(i, lambda: send(mates_sent.at[0], right_got.at[home_slot], 0, user(i)))

    for load in loads[2:]:
        load.wait()
    mates_sent[1] = spread(2)
    mates_sent[2] = spread(3)
    mates_got[pl.ds(my_sub, 1)] = mates_sent[...][None]
    coupling_row = coupling_own[...]
    near = lax.broadcasted_iota(jnp.int32, (depth, depth), 0) == lax.broadcasted_iota(
        jnp.int32, (depth, depth), 1
    )

    def coefficient(i):
        return jnp.sum(jnp.where(near, coupling_row[i : i + 1], 0.0), axis=1, keepdims=True)

    def joined(ref, count):
        return jnp.concatenate(
            [sum(ref[i * pack + j] for j in range(pack)) for i in range(count // pack)], axis=1
        )

    arrived(left_got, cols_count - 1, recv_sem.at[1])
    left_rows = joined(left_got, cols_count)
    left_terms = jnp.dot(
        left_rows.astype(jnp.bfloat16), ladder_own[...], preferred_element_type=jnp.float32
    )
    for i in range(rows_count // pack):
        left_part[i] = left_terms[:, i * LANES : (i + 1) * LANES]

    for i in (*range(1, rows_count), 0):
        chunk = lax.div(lax.rem(home_slot + i, rows_count), pack)
        unless_me(
            i, lambda: send(left_part.at[chunk], left_part_got.at[my_row], 2, holder(i))
        )

    for i in range(pack - 1):
        mate = me - my_sub + lax.rem(my_sub + i + 1, pack)
        send(mates_sent, mates_got.at[my_sub], 5, mate)

    @pl.when(at_home)
    def _():
        left_part_got[pl.ds(my_row, 1)] = left_part[pl.ds(lax.div(home_slot, pack), 1)]
        arrived(right_got, rows_count - 1, recv_sem.at[0])

    @pl.when(jnp.logical_not(at_home))
    def _():
        arrived(right_got, rows_count, recv_sem.at[0])

    right_cols = joined(right_got, rows_count)
    right_terms = lax.dot_general(
        right_cols.astype(jnp.bfloat16),
        ladder_own[...],
        (((1,), (1,)), ((), ())),
        preferred_element_type=jnp.float32,
    )
    for i in range(cols_count // pack):
        right_part[i] = right_terms[:, i * LANES : (i + 1) * LANES]

    for i in range(cols_count - 1):
        chunk = lax.div(lax.rem(my_col + i + 1, cols_count), pack)
        send(right_part.at[chunk], right_part_got.at[my_col], 3, peer(i))
    right_part_got[pl.ds(my_col, 1)] = right_part[pl.ds(lax.div(my_col, pack), 1)]

    def inner(first, second):
        return jnp.sum(first * second, axis=1, keepdims=True)

    def fitted(product, square):
        usable = square > SMALLEST_SQUARE
        return jnp.where(usable, product / jnp.where(usable, square, 1.0), 0.0)

    arrived(mates_got, pack - 1, recv_sem.at[5])
    right, prev_right, prev_left = (
        sum(mates_got[i, j] for i in range(pack)) for j in range(3)
    )
    first_col = my_col - my_sub
    left = sum(left_got[first_col + i] for i in range(pack))
    right_square = inner(right, right)
    left_square = inner(left, left)
    left_right = inner(left, right)

    arrived(right_part_got, cols_count - 1, recv_sem.at[3])
    image_right = jnp.sum(right_part_got[...], axis=0)
    alpha_part = inner(left, image_right)
    right_base = image_right - coefficient(1) * prev_right
    right_fit = fitted(inner(right_base, right), right_square)
    right_rest = right_base - right_fit * right

    @pl.when(at_home)
    def _():
        arrived(left_part_got, rows_count - 1, recv_sem.at[2])

    @pl.when(jnp.logical_not(at_home))
    def _():
        arrived(left_part_got, rows_count, recv_sem.at[2])

    left_base = jnp.sum(left_part_got[...], axis=0) - coefficient(0) * prev_left
    left_fit = fitted(inner(left_base, left), left_square)
    left_rest = left_base - left_fit * left

    sums_sent[...] = to_lanes(
        [
            alpha_part,
            right_fit,
            left_fit,
            inner(right_rest, right_rest),
            inner(right_rest, right),
            right_square,
            inner(left_rest, left_rest),
            inner(left_rest, left),
            left_square,
            inner(left_rest, right_rest),
            inner(left_rest, right),
            inner(left, right_rest),
            left_right,
        ]
    )
    low = my_group < groups // 2

    def far_first(i):
        down = groups - 1 - i
        down = down - (down <= my_group).astype(jnp.int32)
        up = i + (i >= my_group).astype(jnp.int32)
        return jnp.where(low, down, up) * pack + my_sub

    each(
        groups - 1,
        lambda i: send(sums_sent, sums_got.at[pl.ds(my_group, 1)], 4, far_first(i)),
    )
    sums_got[pl.ds(my_group, 1)] = sums_sent[...]

    arrived(right_got, rows_count - 1, send_sem.at[0])
    arrived(left_got, cols_count - 1, send_sem.at[1])
    arrived(left_part_got, rows_count - 1, send_sem.at[2])
    arrived(right_part_got, cols_count - 1, send_sem.at[3])
    arrived(mates_got, pack - 1, send_sem.at[5])

    @pl.when(jnp.logical_not(at_home))
    def _():
        arrived(right_got, 1, send_sem.at[0])
        arrived(left_part_got, 1, send_sem.at[2])

    arrived(sums_got, groups - 1, recv_sem.at[4])
    sums = sums_got[...]

    def value(i):
        return pltpu.roll(sums, LANES - i * depth, 1)

    def total(values):
        return jnp.sum(values, axis=0, keepdims=True) / pairs_total

    alpha_row = total(sums)
    right_off = value(1) - alpha_row
    left_off = value(2) - alpha_row
    right_norm = to_column(
        total(value(3) + right_off * (2.0 * value(4) + right_off * value(5))), 0
    )
    left_norm = to_column(total(value(6) + left_off * (2.0 * value(7) + left_off * value(8))), 0)
    omega_val = to_column(
        total(
            value(9)
            + right_off * value(10)
            + left_off * value(11)
            + right_off * left_off * value(12)
        ),
        0,
    )
    alpha_now = to_column(alpha_row, 0)
    right_res = right_base - alpha_now * right
    left_res = left_base - alpha_now * left
    safe_omega = jnp.maximum(jnp.abs(omega_val), 0.1 * jnp.sqrt(right_norm * left_norm + 1e-06))
    beta_new = jnp.sqrt(safe_omega)
    gamma_new = omega_val / beta_new

    def own_part(array):
        out = array[:, :share]
        for i in range(1, pack):
            out = jnp.where(
                my_sub == i, array[:, i * share : (i + 1) * share], out
            )
        return out

    next_right_out[...] = own_part(right_res / beta_new)
    next_left_out[...] = own_part(left_res * (gamma_new / safe_omega))
    coefficients_out[0:1] = alpha_row[:, :depth]
    coefficients_out[1:2] = to_lanes([beta_new])[:, :depth]
    coefficients_out[2:3] = to_lanes([gamma_new])[:, :depth]
    arrived(sums_got, groups - 1, send_sem.at[4])


def store(a_in, b_in, c_in, a_out, b_out, c_out, sem):
    copies = [
        pltpu.make_async_copy(src, dst, sem.at[i])
        for i, (src, dst) in enumerate(((a_in, a_out), (b_in, b_out), (c_in, c_out)))
    ]
    for copy in copies:
        copy.start()
    for copy in copies:
        copy.wait()


def local(rows_count, cols_count, right, left, prev_right, prev_left, coupling, ladder):
    depth, share = right.shape
    devices = rows_count * cols_count
    pack = LANES // share
    f32 = jnp.float32

    def tiles(count):
        return pltpu.VMEM((count, depth, LANES), f32)

    results = pl.pallas_call(
        functools.partial(kernel, rows_count, cols_count),
        out_shape=(
            pltpu.VMEM(right.shape, f32),
            pltpu.VMEM(left.shape, f32),
            pltpu.VMEM((3, depth), f32),
        ),
        in_specs=[pl.BlockSpec(memory_space=pltpu.HBM)] * 6,
        out_specs=(pl.BlockSpec(memory_space=pltpu.VMEM),) * 3,
        scratch_shapes=[
            pltpu.VMEM((4, depth, share), f32),
            pltpu.VMEM(coupling.shape, f32),
            pltpu.VMEM(ladder.shape, ladder.dtype),
            tiles(1),
            tiles(3),
            tiles(rows_count),
            tiles(cols_count),
            pltpu.VMEM((pack, 3, depth, LANES), f32),
            tiles(cols_count // pack),
            tiles(rows_count // pack),
            tiles(cols_count),
            tiles(rows_count),
            pltpu.VMEM((1, LANES), f32),
            pltpu.VMEM((devices // pack, LANES), f32),
            pltpu.SemaphoreType.DMA((6,)),
            pltpu.SemaphoreType.DMA((6,)),
            pltpu.SemaphoreType.DMA((6,)),
        ],
        compiler_params=pltpu.CompilerParams(
            collective_id=0, has_side_effects=True, vmem_limit_bytes=32 * 1024 * 1024
        ),
    )(*(pltpu.with_memory_space_constraint(x, pltpu.HBM) for x in (right, left, prev_right, prev_left, coupling, ladder)))
    return pl.pallas_call(
        store,
        out_shape=tuple(jax.ShapeDtypeStruct(x.shape, x.dtype) for x in results),
        in_specs=[pl.BlockSpec(memory_space=pltpu.VMEM)] * 3,
        out_specs=(pl.BlockSpec(memory_space=pltpu.HBM),) * 3,
        scratch_shapes=[pltpu.SemaphoreType.DMA((3,))],
        compiler_params=pltpu.CompilerParams(vmem_limit_bytes=1024 * 1024),
    )(*(pltpu.with_memory_space_constraint(x, pltpu.VMEM) for x in results))


def solution(mesh):
    vector = P(None, ("row", "col"))
    return jax.shard_map(
        functools.partial(local, mesh.shape["row"], mesh.shape["col"]),
        mesh=mesh,
        in_specs=(vector, vector, vector, vector, P(), P("row", "col")),
        out_specs=(vector, vector, P()),
        check_vma=False,
    )
```

```python
import functools

import jax
import jax.numpy as jnp
from jax import lax
from jax.experimental import pallas as pl
from jax.experimental.pallas import tpu as pltpu
from jax.sharding import PartitionSpec as P

LOGICAL = pl.DeviceIdType.LOGICAL
LANES = 128
UNROLL_MOST = 32
SMALLEST_SQUARE = 1e-12


def each(count, body):
    if count <= UNROLL_MOST:
        for i in range(count):
            body(i)
    else:
        lax.fori_loop(0, count, lambda i, carry: (body(i), carry)[1], 0)


def arrived(ref, count, sem):
    part = ref.at[pl.ds(0, count)]
    pltpu.make_async_copy(part, part, sem).wait()


def kernel(
    rows_count,
    cols_count,
    right_in,
    left_in,
    prev_right_in,
    prev_left_in,
    coupling_in,
    ladder_in,
    next_right_out,
    next_left_out,
    coefficients_out,
    vectors_own,
    coupling_own,
    ladder_own,
    ladder_turned,
    left_sent,
    mates_sent,
    right_got,
    left_got,
    mates_got,
    right_part,
    left_part,
    right_part_got,
    left_part_got,
    sums_sent,
    sums_got,
    load_sem,
    send_sem,
    recv_sem,
):
    devices = rows_count * cols_count
    depth, share = right_in.shape
    pack = LANES // share
    pairs_total = share * devices
    my_row = lax.axis_index("row")
    my_col = lax.axis_index("col")
    me = my_row * cols_count + my_col
    home_col = lax.div(me, rows_count)
    home_slot = lax.rem(me, rows_count)
    at_home = home_col == my_col

    groups = devices // pack
    my_group = lax.div(me, pack)
    my_sub = lax.rem(me, pack)
    loads = [
        pltpu.make_async_copy(src, dst, load_sem.at[i])
        for i, (src, dst) in enumerate(
            (
                (right_in, vectors_own.at[0]),
                (left_in, vectors_own.at[1]),
                (prev_right_in, vectors_own.at[2]),
                (prev_left_in, vectors_own.at[3]),
                (coupling_in, coupling_own),
                (ladder_in, ladder_own),
            )
        )
    ]
    row_start = my_row * cols_count

    def peer(i):
        return row_start + lax.rem(my_col + i + 1, cols_count)

    def holder(i):
        return my_col * rows_count + lax.rem(home_slot + i, rows_count)

    def user(i):
        return lax.rem(my_row + i, rows_count) * cols_count + home_col

    def unless_me(i, go):
        if i == 0:
            pl.when(jnp.logical_not(at_home))(go)
        else:
            go()

    barrier = pltpu.get_barrier_semaphore()

    def greet(device):
        pl.semaphore_signal(barrier, inc=1, device_id=device, device_id_type=LOGICAL)

    for i in range(cols_count - 1):
        greet(peer(i))
    for load in loads[:2]:
        load.start()
    for i in range(rows_count):
        unless_me(i, lambda: greet(holder(i)))
    for i in range(rows_count):
        unless_me(i, lambda: greet(user(i)))
    for load in loads[2:]:
        load.start()

    lane = lax.broadcasted_iota(jnp.int32, (depth, LANES), 1)
    sub = lax.broadcasted_iota(jnp.int32, (depth, LANES), 0)

    mine = lane // share == my_sub

    def spread(i):
        return jnp.where(mine, jnp.concatenate([vectors_own[i]] * pack, axis=1), 0.0)

    def to_lanes(columns):
        row = jnp.zeros((depth, LANES), jnp.float32)
        for i, column in enumerate(columns):
            row = row + jnp.where(lane == sub + i * depth, column, 0.0)
        return jnp.sum(row, axis=0, keepdims=True)

    def to_column(row, i):
        return jnp.sum(jnp.where(lane == sub + i * depth, row, 0.0), axis=1, keepdims=True)

    for load in loads[:2]:
        load.wait()
    right_own = spread(0)
    left_own = spread(1)
    mates_sent[0] = right_own
    left_sent[0] = left_own
    left_got[pl.ds(my_col, 1)] = left_own[None]

    @pl.when(at_home)
    def _():
        right_got[pl.ds(home_slot, 1)] = right_own[None]

    pl.semaphore_wait(barrier, 2 * rows_count + cols_count - 1 - 2 * at_home.astype(jnp.int32))

    def send(src, dst, sems, device):
        pltpu.make_async_remote_copy(
            src_ref=src,
            dst_ref=dst,
            send_sem=send_sem.at[sems],
            recv_sem=recv_sem.at[sems],
            device_id=device,
            device_id_type=LOGICAL,
        ).start()

    for i in range(cols_count - 1):
        send(left_sent.at[0], left_got.at[my_col], 1, peer(i))
    for i in (*range(1, rows_count), 0):
        unless_me(i, lambda: send(mates_sent.at[0], right_got.at[home_slot], 0, user(i)))

    for load in loads[2:]:
        load.wait()
    mates_sent[1] = spread(2)
    mates_sent[2] = spread(3)
    mates_got[pl.ds(my_sub, 1)] = mates_sent[...][None]
    coupling_row = coupling_own[...]
    near = lax.broadcasted_iota(jnp.int32, (depth, depth), 0) == lax.broadcasted_iota(
        jnp.int32, (depth, depth), 1
    )

    def coefficient(i):
        return jnp.sum(jnp.where(near, coupling_row[i : i + 1], 0.0), axis=1, keepdims=True)

    def joined(ref, count):
        return jnp.concatenate(
            [sum(ref[i * pack + j] for j in range(pack)) for i in range(count // pack)], axis=1
        )

    arrived(left_got, cols_count - 1, recv_sem.at[1])
    left_rows = joined(left_got, cols_count)
    left_terms = jnp.dot(
        left_rows.astype(jnp.bfloat16), ladder_own[...], preferred_element_type=jnp.float32
    )
    for i in range(rows_count // pack):
        left_part[i] = left_terms[:, i * LANES : (i + 1) * LANES]

    for i in (*range(1, rows_count), 0):
        chunk = lax.div(lax.rem(home_slot + i, rows_count), pack)
        unless_me(
            i, lambda: send(left_part.at[chunk], left_part_got.at[my_row], 2, holder(i))
        )

    for i in range(pack - 1):
        mate = me - my_sub + lax.rem(my_sub + i + 1, pack)
        send(mates_sent, mates_got.at[my_sub], 5, mate)
    ladder_turned[...] = ladder_own[...].T

    @pl.when(at_home)
    def _():
        left_part_got[pl.ds(my_row, 1)] = left_part[pl.ds(lax.div(home_slot, pack), 1)]
        arrived(right_got, rows_count - 1, recv_sem.at[0])

    @pl.when(jnp.logical_not(at_home))
    def _():
        arrived(right_got, rows_count, recv_sem.at[0])

    right_cols = joined(right_got, rows_count)
    right_terms = jnp.dot(
        right_cols.astype(jnp.bfloat16), ladder_turned[...], preferred_element_type=jnp.float32
    )
    for i in range(cols_count // pack):
        right_part[i] = right_terms[:, i * LANES : (i + 1) * LANES]

    for i in range(cols_count - 1):
        chunk = lax.div(lax.rem(my_col + i + 1, cols_count), pack)
        send(right_part.at[chunk], right_part_got.at[my_col], 3, peer(i))
    right_part_got[pl.ds(my_col, 1)] = right_part[pl.ds(lax.div(my_col, pack), 1)]

    def inner(first, second):
        return jnp.sum(first * second, axis=1, keepdims=True)

    def inverse(square):
        usable = square > SMALLEST_SQUARE
        return jnp.where(usable, 1.0 / jnp.where(usable, square, 1.0), 0.0)

    arrived(mates_got, pack - 1, recv_sem.at[5])
    right, prev_right, prev_left = (
        sum(mates_got[i, j] for i in range(pack)) for j in range(3)
    )
    first_col = my_col - my_sub
    left = sum(left_got[first_col + i] for i in range(pack))
    right_square = inner(right, right)
    left_square = inner(left, left)
    left_right = inner(left, right)
    right_inverse = inverse(right_square)
    left_inverse = inverse(left_square)

    arrived(right_part_got, cols_count - 1, recv_sem.at[3])
    image_right = jnp.sum(right_part_got[...], axis=0)
    alpha_part = inner(left, image_right)
    right_base = image_right - coefficient(1) * prev_right
    right_fit = inner(right_base, right) * right_inverse
    right_rest = right_base - right_fit * right

    @pl.when(at_home)
    def _():
        arrived(left_part_got, rows_count - 1, recv_sem.at[2])

    @pl.when(jnp.logical_not(at_home))
    def _():
        arrived(left_part_got, rows_count, recv_sem.at[2])

    left_base = jnp.sum(left_part_got[...], axis=0) - coefficient(0) * prev_left
    left_fit = inner(left_base, left) * left_inverse
    left_rest = left_base - left_fit * left

    sums_sent[...] = to_lanes(
        [
            alpha_part,
            right_fit,
            left_fit,
            inner(right_rest, right_rest),
            inner(right_rest, right),
            right_square,
            inner(left_rest, left_rest),
            inner(left_rest, left),
            left_square,
            inner(left_rest, right_rest),
            inner(left_rest, right),
            inner(left, right_rest),
            left_right,
        ]
    )
    low = my_group < groups // 2

    def far_first(i):
        down = groups - 1 - i
        down = down - (down <= my_group).astype(jnp.int32)
        up = i + (i >= my_group).astype(jnp.int32)
        return jnp.where(low, down, up) * pack + my_sub

    each(
        groups - 1,
        lambda i: send(sums_sent, sums_got.at[pl.ds(my_group, 1)], 4, far_first(i)),
    )
    sums_got[pl.ds(my_group, 1)] = sums_sent[...]

    arrived(right_got, rows_count - 1, send_sem.at[0])
    arrived(left_got, cols_count - 1, send_sem.at[1])
    arrived(left_part_got, rows_count - 1, send_sem.at[2])
    arrived(right_part_got, cols_count - 1, send_sem.at[3])
    arrived(mates_got, pack - 1, send_sem.at[5])

    @pl.when(jnp.logical_not(at_home))
    def _():
        arrived(right_got, 1, send_sem.at[0])
        arrived(left_part_got, 1, send_sem.at[2])

    arrived(sums_got, groups - 1, recv_sem.at[4])
    sums = sums_got[...]

    def value(i):
        return pltpu.roll(sums, LANES - i * depth, 1)

    def total(values):
        return jnp.sum(values, axis=0, keepdims=True) / pairs_total

    alpha_row = total(sums)
    right_off = value(1) - alpha_row
    left_off = value(2) - alpha_row
    right_norm = to_column(
        total(value(3) + right_off * (2.0 * value(4) + right_off * value(5))), 0
    )
    left_norm = to_column(total(value(6) + left_off * (2.0 * value(7) + left_off * value(8))), 0)
    omega_val = to_column(
        total(
            value(9)
            + right_off * value(10)
            + left_off * value(11)
            + right_off * left_off * value(12)
        ),
        0,
    )
    alpha_now = to_column(alpha_row, 0)
    right_res = right_base - alpha_now * right
    left_res = left_base - alpha_now * left
    safe_omega = jnp.maximum(jnp.abs(omega_val), 0.1 * jnp.sqrt(right_norm * left_norm + 1e-06))
    beta_new = jnp.sqrt(safe_omega)
    gamma_new = omega_val / beta_new

    def own_part(array):
        out = array[:, :share]
        for i in range(1, pack):
            out = jnp.where(
                my_sub == i, array[:, i * share : (i + 1) * share], out
            )
        return out

    next_right_out[...] = own_part(right_res / beta_new)
    next_left_out[...] = own_part(left_res * (gamma_new / safe_omega))
    coefficients_out[0:1] = alpha_row[:, :depth]
    coefficients_out[1:2] = to_lanes([beta_new])[:, :depth]
    coefficients_out[2:3] = to_lanes([gamma_new])[:, :depth]
    arrived(sums_got, groups - 1, send_sem.at[4])


def store(a_in, b_in, c_in, a_out, b_out, c_out, sem):
    copies = [
        pltpu.make_async_copy(src, dst, sem.at[i])
        for i, (src, dst) in enumerate(((a_in, a_out), (b_in, b_out), (c_in, c_out)))
    ]
    for copy in copies:
        copy.start()
    for copy in copies:
        copy.wait()


def local(rows_count, cols_count, right, left, prev_right, prev_left, coupling, ladder):
    depth, share = right.shape
    devices = rows_count * cols_count
    pack = LANES // share
    f32 = jnp.float32

    def tiles(count):
        return pltpu.VMEM((count, depth, LANES), f32)

    results = pl.pallas_call(
        functools.partial(kernel, rows_count, cols_count),
        out_shape=(
            pltpu.VMEM(right.shape, f32),
            pltpu.VMEM(left.shape, f32),
            pltpu.VMEM((3, depth), f32),
        ),
        in_specs=[pl.BlockSpec(memory_space=pltpu.HBM)] * 6,
        out_specs=(pl.BlockSpec(memory_space=pltpu.VMEM),) * 3,
        scratch_shapes=[
            pltpu.VMEM((4, depth, share), f32),
            pltpu.VMEM(coupling.shape, f32),
            pltpu.VMEM(ladder.shape, ladder.dtype),
            pltpu.VMEM(ladder.shape[::-1], ladder.dtype),
            tiles(1),
            tiles(3),
            tiles(rows_count),
            tiles(cols_count),
            pltpu.VMEM((pack, 3, depth, LANES), f32),
            tiles(cols_count // pack),
            tiles(rows_count // pack),
            tiles(cols_count),
            tiles(rows_count),
            pltpu.VMEM((1, LANES), f32),
            pltpu.VMEM((devices // pack, LANES), f32),
            pltpu.SemaphoreType.DMA((6,)),
            pltpu.SemaphoreType.DMA((6,)),
            pltpu.SemaphoreType.DMA((6,)),
        ],
        compiler_params=pltpu.CompilerParams(
            collective_id=0, has_side_effects=True, vmem_limit_bytes=32 * 1024 * 1024
        ),
    )(*(pltpu.with_memory_space_constraint(x, pltpu.HBM) for x in (right, left, prev_right, prev_left, coupling, ladder)))
    return pl.pallas_call(
        store,
        out_shape=tuple(jax.ShapeDtypeStruct(x.shape, x.dtype) for x in results),
        in_specs=[pl.BlockSpec(memory_space=pltpu.VMEM)] * 3,
        out_specs=(pl.BlockSpec(memory_space=pltpu.HBM),) * 3,
        scratch_shapes=[pltpu.SemaphoreType.DMA((3,))],
        compiler_params=pltpu.CompilerParams(vmem_limit_bytes=1024 * 1024),
    )(*(pltpu.with_memory_space_constraint(x, pltpu.VMEM) for x in results))


def solution(mesh):
    vector = P(None, ("row", "col"))
    return jax.shard_map(
        functools.partial(local, mesh.shape["row"], mesh.shape["col"]),
        mesh=mesh,
        in_specs=(vector, vector, vector, vector, P(), P("row", "col")),
        out_specs=(vector, vector, P()),
        check_vma=False,
    )
```

```python
import functools

import jax
import jax.numpy as jnp
from jax import lax
from jax.experimental import pallas as pl
from jax.experimental.pallas import tpu as pltpu
from jax.sharding import PartitionSpec as P

LOGICAL = pl.DeviceIdType.LOGICAL
LANES = 128
LAYERS = 4
UNROLL_MOST = 32
SMALLEST_SQUARE = 1e-12


def each(count, body):
    if count <= UNROLL_MOST:
        for i in range(count):
            body(i)
    else:
        lax.fori_loop(0, count, lambda i, carry: (body(i), carry)[1], 0)


def arrived(ref, count, sem):
    part = ref.at[pl.ds(0, count)]
    pltpu.make_async_copy(part, part, sem).wait()


def kernel(
    rows_count,
    cols_count,
    right_in,
    left_in,
    prev_right_in,
    prev_left_in,
    coupling_in,
    ladder_in,
    next_right_out,
    next_left_out,
    coefficients_out,
    vectors_own,
    coupling_own,
    ladder_own,
    ladder_turned,
    left_sent,
    mates_sent,
    right_got,
    left_got,
    mates_got,
    right_part,
    left_part,
    right_part_got,
    left_part_got,
    sums_sent,
    sums_got,
    load_sem,
    send_sem,
    recv_sem,
):
    devices = rows_count * cols_count
    depth, share = right_in.shape
    pack = LANES // share
    pairs_total = share * devices
    my_row = lax.axis_index("row")
    my_col = lax.axis_index("col")
    me = my_row * cols_count + my_col
    home_col = lax.div(me, rows_count)
    home_slot = lax.rem(me, rows_count)
    at_home = home_col == my_col

    layers = LAYERS if rows_count % LAYERS == 0 else 1
    span = rows_count // layers
    layer = lax.div(my_row, span)
    above = layer > lax.div(lax.div(my_col * rows_count, cols_count), span)
    first_half = my_row < rows_count // 2

    groups = devices // pack
    my_group = lax.div(me, pack)
    my_sub = lax.rem(me, pack)
    loads = [
        pltpu.make_async_copy(src, dst, load_sem.at[i])
        for i, (src, dst) in enumerate(
            (
                (right_in, vectors_own.at[0]),
                (left_in, vectors_own.at[1]),
                (prev_right_in, vectors_own.at[2]),
                (prev_left_in, vectors_own.at[3]),
                (coupling_in, coupling_own),
                (ladder_in, ladder_own),
            )
        )
    ]
    row_start = my_row * cols_count

    def peer(i):
        return row_start + lax.rem(my_col + i + 1, cols_count)

    def holder(i):
        return my_col * rows_count + lax.rem(home_slot + i, rows_count)

    def user(i):
        step = jnp.where(first_half, rows_count - i, i)
        return lax.rem(my_row + step, rows_count) * cols_count + home_col

    def unless_me(i, go):
        if i == 0:
            pl.when(jnp.logical_not(at_home))(go)
        else:
            go()

    barrier = pltpu.get_barrier_semaphore()

    def greet(device):
        pl.semaphore_signal(barrier, inc=1, device_id=device, device_id_type=LOGICAL)

    for load in loads[:2]:
        load.start()
    for i in range(rows_count):
        unless_me(i, lambda: greet(holder(i)))
    for i in range(cols_count - 1):
        greet(peer(i))
    for row in range(span, rows_count):
        pl.when(row >= (layer + 1) * span)(
            functools.partial(greet, row * cols_count + home_col)
        )
    for load in loads[2:]:
        load.start()

    lane = lax.broadcasted_iota(jnp.int32, (depth, LANES), 1)
    sub = lax.broadcasted_iota(jnp.int32, (depth, LANES), 0)

    mine = lane // share == my_sub

    def spread(i):
        return jnp.where(mine, jnp.concatenate([vectors_own[i]] * pack, axis=1), 0.0)

    def to_lanes(columns):
        row = jnp.zeros((depth, LANES), jnp.float32)
        for i, column in enumerate(columns):
            row = row + jnp.where(lane == sub + i * depth, column, 0.0)
        return jnp.sum(row, axis=0, keepdims=True)

    def to_column(row, i):
        return jnp.sum(jnp.where(lane == sub + i * depth, row, 0.0), axis=1, keepdims=True)

    for load in loads[:2]:
        load.wait()
    right_own = spread(0)
    left_own = spread(1)
    mates_sent[0] = right_own
    left_sent[0] = left_own
    left_got[pl.ds(my_col, 1)] = left_own[None]

    @pl.when(at_home)
    def _():
        right_got[pl.ds(home_slot, 1)] = right_own[None]

    awaited = rows_count + cols_count - 1 - at_home.astype(jnp.int32)
    pl.semaphore_wait(barrier, awaited + jnp.where(above, rows_count, 0))

    def send(src, dst, sems, device):
        pltpu.make_async_remote_copy(
            src_ref=src,
            dst_ref=dst,
            send_sem=send_sem.at[sems],
            recv_sem=recv_sem.at[sems],
            device_id=device,
            device_id_type=LOGICAL,
        ).start()

    def send_right(i):
        unless_me(i, lambda: send(mates_sent.at[0], right_got.at[home_slot], 0, user(i)))

    for i in range(1, rows_count // 2):
        send_right(i)
    for i in range(cols_count - 1):
        send(left_sent.at[0], left_got.at[my_col], 1, peer(i))
    for i in (*range(rows_count // 2, rows_count), 0):
        send_right(i)

    for load in loads[2:]:
        load.wait()
    mates_sent[1] = spread(2)
    mates_sent[2] = spread(3)
    mates_got[pl.ds(my_sub, 1)] = mates_sent[...][None]
    coupling_row = coupling_own[...]
    near = lax.broadcasted_iota(jnp.int32, (depth, depth), 0) == lax.broadcasted_iota(
        jnp.int32, (depth, depth), 1
    )

    def coefficient(i):
        return jnp.sum(jnp.where(near, coupling_row[i : i + 1], 0.0), axis=1, keepdims=True)

    def joined(ref, count):
        return jnp.concatenate(
            [sum(ref[i * pack + j] for j in range(pack)) for i in range(count // pack)], axis=1
        )

    arrived(left_got, cols_count - 1, recv_sem.at[1])
    left_rows = joined(left_got, cols_count)
    left_terms = jnp.dot(
        left_rows.astype(jnp.bfloat16), ladder_own[...], preferred_element_type=jnp.float32
    )
    for i in range(rows_count // pack):
        left_part[i] = left_terms[:, i * LANES : (i + 1) * LANES]

    def send_left_parts():
        for i in (*range(1, rows_count), 0):
            chunk = lax.div(lax.rem(home_slot + i, rows_count), pack)
            unless_me(
                i, lambda: send(left_part.at[chunk], left_part_got.at[my_row], 2, holder(i))
            )

    pl.when(above)(send_left_parts)
    for i in range(pack - 1):
        mate = me - my_sub + lax.rem(my_sub + i + 1, pack)
        send(mates_sent, mates_got.at[my_sub], 5, mate)
    ladder_turned[...] = ladder_own[...].T

    @pl.when(at_home)
    def _():
        left_part_got[pl.ds(my_row, 1)] = left_part[pl.ds(lax.div(home_slot, pack), 1)]
        arrived(right_got, rows_count - 1, recv_sem.at[0])

    @pl.when(jnp.logical_not(at_home))
    def _():
        arrived(right_got, rows_count, recv_sem.at[0])

    pl.when(jnp.logical_not(above))(send_left_parts)
    right_cols = joined(right_got, rows_count)
    right_terms = jnp.dot(
        right_cols.astype(jnp.bfloat16), ladder_turned[...], preferred_element_type=jnp.float32
    )
    for i in range(cols_count // pack):
        right_part[i] = right_terms[:, i * LANES : (i + 1) * LANES]

    for i in range(cols_count - 1):
        chunk = lax.div(lax.rem(my_col + i + 1, cols_count), pack)
        send(right_part.at[chunk], right_part_got.at[my_col], 3, peer(i))
    right_part_got[pl.ds(my_col, 1)] = right_part[pl.ds(lax.div(my_col, pack), 1)]

    def inner(first, second):
        return jnp.sum(first * second, axis=1, keepdims=True)

    def inverse(square):
        usable = square > SMALLEST_SQUARE
        return jnp.where(usable, 1.0 / jnp.where(usable, square, 1.0), 0.0)

    arrived(mates_got, pack - 1, recv_sem.at[5])
    right, prev_right, prev_left = (
        sum(mates_got[i, j] for i in range(pack)) for j in range(3)
    )
    first_col = my_col - my_sub
    left = sum(left_got[first_col + i] for i in range(pack))
    right_square = inner(right, right)
    left_square = inner(left, left)
    left_right = inner(left, right)
    right_inverse = inverse(right_square)
    left_inverse = inverse(left_square)

    arrived(right_part_got, cols_count - 1, recv_sem.at[3])
    image_right = jnp.sum(right_part_got[...], axis=0)
    alpha_part = inner(left, image_right)
    right_base = image_right - coefficient(1) * prev_right
    right_fit = inner(right_base, right) * right_inverse
    right_rest = right_base - right_fit * right

    @pl.when(at_home)
    def _():
        arrived(left_part_got, rows_count - 1, recv_sem.at[2])

    @pl.when(jnp.logical_not(at_home))
    def _():
        arrived(left_part_got, rows_count, recv_sem.at[2])

    left_base = jnp.sum(left_part_got[...], axis=0) - coefficient(0) * prev_left
    left_fit = inner(left_base, left) * left_inverse
    left_rest = left_base - left_fit * left

    sums_sent[...] = to_lanes(
        [
            alpha_part,
            right_fit,
            left_fit,
            inner(right_rest, right_rest),
            inner(right_rest, right),
            right_square,
            inner(left_rest, left_rest),
            inner(left_rest, left),
            left_square,
            inner(left_rest, right_rest),
            inner(left_rest, right),
            inner(left, right_rest),
            left_right,
        ]
    )
    low = my_group < groups // 2

    def far_first(i):
        down = groups - 1 - i
        down = down - (down <= my_group).astype(jnp.int32)
        up = i + (i >= my_group).astype(jnp.int32)
        return jnp.where(low, down, up) * pack + my_sub

    each(
        groups - 1,
        lambda i: send(sums_sent, sums_got.at[pl.ds(my_group, 1)], 4, far_first(i)),
    )
    sums_got[pl.ds(my_group, 1)] = sums_sent[...]

    arrived(right_got, rows_count - 1, send_sem.at[0])
    arrived(left_got, cols_count - 1, send_sem.at[1])
    arrived(left_part_got, rows_count - 1, send_sem.at[2])
    arrived(right_part_got, cols_count - 1, send_sem.at[3])
    arrived(mates_got, pack - 1, send_sem.at[5])

    @pl.when(jnp.logical_not(at_home))
    def _():
        arrived(right_got, 1, send_sem.at[0])
        arrived(left_part_got, 1, send_sem.at[2])

    arrived(sums_got, groups - 1, recv_sem.at[4])
    sums = sums_got[...]

    def value(i):
        return pltpu.roll(sums, LANES - i * depth, 1)

    def total(values):
        return jnp.sum(values, axis=0, keepdims=True) / pairs_total

    alpha_row = total(sums)
    right_off = value(1) - alpha_row
    left_off = value(2) - alpha_row
    right_norm = to_column(
        total(value(3) + right_off * (2.0 * value(4) + right_off * value(5))), 0
    )
    left_norm = to_column(total(value(6) + left_off * (2.0 * value(7) + left_off * value(8))), 0)
    omega_val = to_column(
        total(
            value(9)
            + right_off * value(10)
            + left_off * value(11)
            + right_off * left_off * value(12)
        ),
        0,
    )
    alpha_now = to_column(alpha_row, 0)
    right_res = right_base - alpha_now * right
    left_res = left_base - alpha_now * left
    safe_omega = jnp.maximum(jnp.abs(omega_val), 0.1 * jnp.sqrt(right_norm * left_norm + 1e-06))
    beta_new = jnp.sqrt(safe_omega)
    gamma_new = omega_val / beta_new

    def own_part(array):
        out = array[:, :share]
        for i in range(1, pack):
            out = jnp.where(
                my_sub == i, array[:, i * share : (i + 1) * share], out
            )
        return out

    next_right_out[...] = own_part(right_res / beta_new)
    next_left_out[...] = own_part(left_res * (gamma_new / safe_omega))
    coefficients_out[0:1] = alpha_row[:, :depth]
    coefficients_out[1:2] = to_lanes([beta_new])[:, :depth]
    coefficients_out[2:3] = to_lanes([gamma_new])[:, :depth]
    arrived(sums_got, groups - 1, send_sem.at[4])


def store(a_in, b_in, c_in, a_out, b_out, c_out, sem):
    copies = [
        pltpu.make_async_copy(src, dst, sem.at[i])
        for i, (src, dst) in enumerate(((a_in, a_out), (b_in, b_out), (c_in, c_out)))
    ]
    for copy in copies:
        copy.start()
    for copy in copies:
        copy.wait()


def local(rows_count, cols_count, right, left, prev_right, prev_left, coupling, ladder):
    depth, share = right.shape
    devices = rows_count * cols_count
    pack = LANES // share
    f32 = jnp.float32

    def tiles(count):
        return pltpu.VMEM((count, depth, LANES), f32)

    results = pl.pallas_call(
        functools.partial(kernel, rows_count, cols_count),
        out_shape=(
            pltpu.VMEM(right.shape, f32),
            pltpu.VMEM(left.shape, f32),
            pltpu.VMEM((3, depth), f32),
        ),
        in_specs=[pl.BlockSpec(memory_space=pltpu.HBM)] * 6,
        out_specs=(pl.BlockSpec(memory_space=pltpu.VMEM),) * 3,
        scratch_shapes=[
            pltpu.VMEM((4, depth, share), f32),
            pltpu.VMEM(coupling.shape, f32),
            pltpu.VMEM(ladder.shape, ladder.dtype),
            pltpu.VMEM(ladder.shape[::-1], ladder.dtype),
            tiles(1),
            tiles(3),
            tiles(rows_count),
            tiles(cols_count),
            pltpu.VMEM((pack, 3, depth, LANES), f32),
            tiles(cols_count // pack),
            tiles(rows_count // pack),
            tiles(cols_count),
            tiles(rows_count),
            pltpu.VMEM((1, LANES), f32),
            pltpu.VMEM((devices // pack, LANES), f32),
            pltpu.SemaphoreType.DMA((6,)),
            pltpu.SemaphoreType.DMA((6,)),
            pltpu.SemaphoreType.DMA((6,)),
        ],
        compiler_params=pltpu.CompilerParams(
            collective_id=0, has_side_effects=True, vmem_limit_bytes=32 * 1024 * 1024
        ),
    )(*(pltpu.with_memory_space_constraint(x, pltpu.HBM) for x in (right, left, prev_right, prev_left, coupling, ladder)))
    return pl.pallas_call(
        store,
        out_shape=tuple(jax.ShapeDtypeStruct(x.shape, x.dtype) for x in results),
        in_specs=[pl.BlockSpec(memory_space=pltpu.VMEM)] * 3,
        out_specs=(pl.BlockSpec(memory_space=pltpu.HBM),) * 3,
        scratch_shapes=[pltpu.SemaphoreType.DMA((3,))],
        compiler_params=pltpu.CompilerParams(vmem_limit_bytes=1024 * 1024),
    )(*(pltpu.with_memory_space_constraint(x, pltpu.VMEM) for x in results))


def solution(mesh):
    vector = P(None, ("row", "col"))
    return jax.shard_map(
        functools.partial(local, mesh.shape["row"], mesh.shape["col"]),
        mesh=mesh,
        in_specs=(vector, vector, vector, vector, P(), P("row", "col")),
        out_specs=(vector, vector, P()),
        check_vma=False,
    )
```

```python
import functools

import jax
import jax.numpy as jnp
from jax import lax
from jax.experimental import pallas as pl
from jax.experimental.pallas import tpu as pltpu
from jax.sharding import PartitionSpec as P

LOGICAL = pl.DeviceIdType.LOGICAL
LANES = 128
LAYERS = 4
UNROLL_MOST = 32
SMALLEST_SQUARE = 1e-12


def each(count, body):
    if count <= UNROLL_MOST:
        for i in range(count):
            body(i)
    else:
        lax.fori_loop(0, count, lambda i, carry: (body(i), carry)[1], 0)


def arrived(ref, count, sem):
    part = ref.at[pl.ds(0, count)]
    pltpu.make_async_copy(part, part, sem).wait()


def kernel(
    rows_count,
    cols_count,
    right_in,
    left_in,
    prev_right_in,
    prev_left_in,
    coupling_in,
    ladder_in,
    next_right_out,
    next_left_out,
    coefficients_out,
    vectors_own,
    coupling_own,
    ladder_own,
    ladder_turned,
    left_sent,
    mates_sent,
    right_got,
    left_got,
    mates_got,
    right_part,
    left_part,
    right_part_got,
    left_part_got,
    sums_sent,
    sums_got,
    load_sem,
    send_sem,
    recv_sem,
):
    devices = rows_count * cols_count
    depth, share = right_in.shape
    pack = LANES // share
    pairs_total = share * devices
    my_row = lax.axis_index("row")
    my_col = lax.axis_index("col")
    me = my_row * cols_count + my_col
    home_col = lax.div(me, rows_count)
    home_slot = lax.rem(me, rows_count)
    at_home = home_col == my_col

    layers = LAYERS if rows_count % LAYERS == 0 else 1
    span = rows_count // layers
    layer = lax.div(my_row, span)
    below = layer < lax.div(lax.div(my_col * rows_count, cols_count), span)
    first_half = my_row < rows_count // 2

    groups = devices // pack
    my_group = lax.div(me, pack)
    my_sub = lax.rem(me, pack)
    loads = [
        pltpu.make_async_copy(src, dst, load_sem.at[i])
        for i, (src, dst) in enumerate(
            (
                (right_in, vectors_own.at[0]),
                (left_in, vectors_own.at[1]),
                (prev_right_in, vectors_own.at[2]),
                (prev_left_in, vectors_own.at[3]),
                (coupling_in, coupling_own),
                (ladder_in, ladder_own),
            )
        )
    ]
    row_start = my_row * cols_count

    def peer(i):
        return row_start + lax.rem(my_col + i + 1, cols_count)

    def holder(i):
        return my_col * rows_count + lax.rem(home_slot + i, rows_count)

    def user(i):
        step = jnp.where(first_half, rows_count - i, i)
        return lax.rem(my_row + step, rows_count) * cols_count + home_col

    def unless_me(i, go):
        if i == 0:
            pl.when(jnp.logical_not(at_home))(go)
        else:
            go()

    barrier = pltpu.get_barrier_semaphore()

    def greet(device):
        pl.semaphore_signal(barrier, inc=1, device_id=device, device_id_type=LOGICAL)

    for i in range(cols_count - 1):
        greet(peer(i))
    for load in loads[:2]:
        load.start()
    for i in range(rows_count):
        unless_me(i, lambda: greet(holder(i)))
    for row in range(rows_count):
        is_me = jnp.logical_and(at_home, my_row == row)
        pl.when(jnp.logical_and(row >= layer * span, jnp.logical_not(is_me)))(
            functools.partial(greet, row * cols_count + home_col)
        )
    for load in loads[2:]:
        load.start()

    lane = lax.broadcasted_iota(jnp.int32, (depth, LANES), 1)
    sub = lax.broadcasted_iota(jnp.int32, (depth, LANES), 0)

    mine = lane // share == my_sub

    def spread(i):
        return jnp.where(mine, jnp.concatenate([vectors_own[i]] * pack, axis=1), 0.0)

    def to_lanes(columns):
        row = jnp.zeros((depth, LANES), jnp.float32)
        for i, column in enumerate(columns):
            row = row + jnp.where(lane == sub + i * depth, column, 0.0)
        return jnp.sum(row, axis=0, keepdims=True)

    def to_column(row, i):
        return jnp.sum(jnp.where(lane == sub + i * depth, row, 0.0), axis=1, keepdims=True)

    for load in loads[:2]:
        load.wait()
    right_own = spread(0)
    left_own = spread(1)
    mates_sent[0] = right_own
    left_sent[0] = left_own
    left_got[pl.ds(my_col, 1)] = left_own[None]

    @pl.when(at_home)
    def _():
        right_got[pl.ds(home_slot, 1)] = right_own[None]

    others = rows_count - at_home.astype(jnp.int32)
    pl.semaphore_wait(barrier, cols_count - 1 + others + jnp.where(below, 0, others))

    def send(src, dst, sems, device):
        pltpu.make_async_remote_copy(
            src_ref=src,
            dst_ref=dst,
            send_sem=send_sem.at[sems],
            recv_sem=recv_sem.at[sems],
            device_id=device,
            device_id_type=LOGICAL,
        ).start()

    def send_right(i):
        unless_me(i, lambda: send(mates_sent.at[0], right_got.at[home_slot], 0, user(i)))

    for i in range(cols_count - 1):
        send(left_sent.at[0], left_got.at[my_col], 1, peer(i))
    for i in (*range(1, rows_count), 0):
        send_right(i)

    for load in loads[2:]:
        load.wait()
    mates_sent[1] = spread(2)
    mates_sent[2] = spread(3)
    mates_got[pl.ds(my_sub, 1)] = mates_sent[...][None]
    coupling_row = coupling_own[...]
    near = lax.broadcasted_iota(jnp.int32, (depth, depth), 0) == lax.broadcasted_iota(
        jnp.int32, (depth, depth), 1
    )

    def coefficient(i):
        return jnp.sum(jnp.where(near, coupling_row[i : i + 1], 0.0), axis=1, keepdims=True)

    def joined(ref, count):
        return jnp.concatenate(
            [sum(ref[i * pack + j] for j in range(pack)) for i in range(count // pack)], axis=1
        )

    arrived(left_got, cols_count - 1, recv_sem.at[1])
    left_rows = joined(left_got, cols_count)
    left_terms = jnp.dot(
        left_rows.astype(jnp.bfloat16), ladder_own[...], preferred_element_type=jnp.float32
    )
    for i in range(rows_count // pack):
        left_part[i] = left_terms[:, i * LANES : (i + 1) * LANES]

    def send_left_parts():
        for i in (*range(1, rows_count), 0):
            chunk = lax.div(lax.rem(home_slot + i, rows_count), pack)
            unless_me(
                i, lambda: send(left_part.at[chunk], left_part_got.at[my_row], 2, holder(i))
            )

    pl.when(jnp.logical_not(below))(send_left_parts)
    for i in range(pack - 1):
        mate = me - my_sub + lax.rem(my_sub + i + 1, pack)
        send(mates_sent, mates_got.at[my_sub], 5, mate)
    ladder_turned[...] = ladder_own[...].T

    @pl.when(at_home)
    def _():
        left_part_got[pl.ds(my_row, 1)] = left_part[pl.ds(lax.div(home_slot, pack), 1)]
        arrived(right_got, rows_count - 1, recv_sem.at[0])

    @pl.when(jnp.logical_not(at_home))
    def _():
        arrived(right_got, rows_count, recv_sem.at[0])

    pl.when(below)(send_left_parts)
    right_cols = joined(right_got, rows_count)
    right_terms = jnp.dot(
        right_cols.astype(jnp.bfloat16), ladder_turned[...], preferred_element_type=jnp.float32
    )
    for i in range(cols_count // pack):
        right_part[i] = right_terms[:, i * LANES : (i + 1) * LANES]

    for i in range(cols_count - 1):
        chunk = lax.div(lax.rem(my_col + i + 1, cols_count), pack)
        send(right_part.at[chunk], right_part_got.at[my_col], 3, peer(i))
    right_part_got[pl.ds(my_col, 1)] = right_part[pl.ds(lax.div(my_col, pack), 1)]

    def inner(first, second):
        return jnp.sum(first * second, axis=1, keepdims=True)

    def inverse(square):
        usable = square > SMALLEST_SQUARE
        return jnp.where(usable, 1.0 / jnp.where(usable, square, 1.0), 0.0)

    arrived(mates_got, pack - 1, recv_sem.at[5])
    right, prev_right, prev_left = (
        sum(mates_got[i, j] for i in range(pack)) for j in range(3)
    )
    first_col = my_col - my_sub
    left = sum(left_got[first_col + i] for i in range(pack))
    right_square = inner(right, right)
    left_square = inner(left, left)
    left_right = inner(left, right)
    right_inverse = inverse(right_square)
    left_inverse = inverse(left_square)

    arrived(right_part_got, cols_count - 1, recv_sem.at[3])
    image_right = jnp.sum(right_part_got[...], axis=0)
    alpha_part = inner(left, image_right)
    right_base = image_right - coefficient(1) * prev_right
    right_fit = inner(right_base, right) * right_inverse
    right_rest = right_base - right_fit * right

    @pl.when(at_home)
    def _():
        arrived(left_part_got, rows_count - 1, recv_sem.at[2])

    @pl.when(jnp.logical_not(at_home))
    def _():
        arrived(left_part_got, rows_count, recv_sem.at[2])

    left_base = jnp.sum(left_part_got[...], axis=0) - coefficient(0) * prev_left
    left_fit = inner(left_base, left) * left_inverse
    left_rest = left_base - left_fit * left

    sums_sent[...] = to_lanes(
        [
            alpha_part,
            right_fit,
            left_fit,
            inner(right_rest, right_rest),
            inner(right_rest, right),
            right_square,
            inner(left_rest, left_rest),
            inner(left_rest, left),
            left_square,
            inner(left_rest, right_rest),
            inner(left_rest, right),
            inner(left, right_rest),
            left_right,
        ]
    )
    low = my_group < groups // 2

    def far_first(i):
        down = groups - 1 - i
        down = down - (down <= my_group).astype(jnp.int32)
        up = i + (i >= my_group).astype(jnp.int32)
        return jnp.where(low, down, up) * pack + my_sub

    each(
        groups - 1,
        lambda i: send(sums_sent, sums_got.at[pl.ds(my_group, 1)], 4, far_first(i)),
    )
    sums_got[pl.ds(my_group, 1)] = sums_sent[...]

    arrived(right_got, rows_count - 1, send_sem.at[0])
    arrived(left_got, cols_count - 1, send_sem.at[1])
    arrived(left_part_got, rows_count - 1, send_sem.at[2])
    arrived(right_part_got, cols_count - 1, send_sem.at[3])
    arrived(mates_got, pack - 1, send_sem.at[5])

    @pl.when(jnp.logical_not(at_home))
    def _():
        arrived(right_got, 1, send_sem.at[0])
        arrived(left_part_got, 1, send_sem.at[2])

    arrived(sums_got, groups - 1, recv_sem.at[4])
    sums = sums_got[...]

    def value(i):
        return pltpu.roll(sums, LANES - i * depth, 1)

    def total(values):
        return jnp.sum(values, axis=0, keepdims=True) / pairs_total

    alpha_row = total(sums)
    right_off = value(1) - alpha_row
    left_off = value(2) - alpha_row
    right_norm = to_column(
        total(value(3) + right_off * (2.0 * value(4) + right_off * value(5))), 0
    )
    left_norm = to_column(total(value(6) + left_off * (2.0 * value(7) + left_off * value(8))), 0)
    omega_val = to_column(
        total(
            value(9)
            + right_off * value(10)
            + left_off * value(11)
            + right_off * left_off * value(12)
        ),
        0,
    )
    alpha_now = to_column(alpha_row, 0)
    right_res = right_base - alpha_now * right
    left_res = left_base - alpha_now * left
    safe_omega = jnp.maximum(jnp.abs(omega_val), 0.1 * jnp.sqrt(right_norm * left_norm + 1e-06))
    beta_new = jnp.sqrt(safe_omega)
    gamma_new = omega_val / beta_new

    def own_part(array):
        out = array[:, :share]
        for i in range(1, pack):
            out = jnp.where(
                my_sub == i, array[:, i * share : (i + 1) * share], out
            )
        return out

    next_right_out[...] = own_part(right_res / beta_new)
    next_left_out[...] = own_part(left_res * (gamma_new / safe_omega))
    coefficients_out[0:1] = alpha_row[:, :depth]
    coefficients_out[1:2] = to_lanes([beta_new])[:, :depth]
    coefficients_out[2:3] = to_lanes([gamma_new])[:, :depth]
    arrived(sums_got, groups - 1, send_sem.at[4])


def store(a_in, b_in, c_in, a_out, b_out, c_out, sem):
    copies = [
        pltpu.make_async_copy(src, dst, sem.at[i])
        for i, (src, dst) in enumerate(((a_in, a_out), (b_in, b_out), (c_in, c_out)))
    ]
    for copy in copies:
        copy.start()
    for copy in copies:
        copy.wait()


def local(rows_count, cols_count, right, left, prev_right, prev_left, coupling, ladder):
    depth, share = right.shape
    devices = rows_count * cols_count
    pack = LANES // share
    f32 = jnp.float32

    def tiles(count):
        return pltpu.VMEM((count, depth, LANES), f32)

    results = pl.pallas_call(
        functools.partial(kernel, rows_count, cols_count),
        out_shape=(
            pltpu.VMEM(right.shape, f32),
            pltpu.VMEM(left.shape, f32),
            pltpu.VMEM((3, depth), f32),
        ),
        in_specs=[pl.BlockSpec(memory_space=pltpu.HBM)] * 6,
        out_specs=(pl.BlockSpec(memory_space=pltpu.VMEM),) * 3,
        scratch_shapes=[
            pltpu.VMEM((4, depth, share), f32),
            pltpu.VMEM(coupling.shape, f32),
            pltpu.VMEM(ladder.shape, ladder.dtype),
            pltpu.VMEM(ladder.shape[::-1], ladder.dtype),
            tiles(1),
            tiles(3),
            tiles(rows_count),
            tiles(cols_count),
            pltpu.VMEM((pack, 3, depth, LANES), f32),
            tiles(cols_count // pack),
            tiles(rows_count // pack),
            tiles(cols_count),
            tiles(rows_count),
            pltpu.VMEM((1, LANES), f32),
            pltpu.VMEM((devices // pack, LANES), f32),
            pltpu.SemaphoreType.DMA((6,)),
            pltpu.SemaphoreType.DMA((6,)),
            pltpu.SemaphoreType.DMA((6,)),
        ],
        compiler_params=pltpu.CompilerParams(
            collective_id=0, has_side_effects=True, vmem_limit_bytes=32 * 1024 * 1024
        ),
    )(*(pltpu.with_memory_space_constraint(x, pltpu.HBM) for x in (right, left, prev_right, prev_left, coupling, ladder)))
    return pl.pallas_call(
        store,
        out_shape=tuple(jax.ShapeDtypeStruct(x.shape, x.dtype) for x in results),
        in_specs=[pl.BlockSpec(memory_space=pltpu.VMEM)] * 3,
        out_specs=(pl.BlockSpec(memory_space=pltpu.HBM),) * 3,
        scratch_shapes=[pltpu.SemaphoreType.DMA((3,))],
        compiler_params=pltpu.CompilerParams(vmem_limit_bytes=1024 * 1024),
    )(*(pltpu.with_memory_space_constraint(x, pltpu.VMEM) for x in results))


def solution(mesh):
    vector = P(None, ("row", "col"))
    return jax.shard_map(
        functools.partial(local, mesh.shape["row"], mesh.shape["col"]),
        mesh=mesh,
        in_specs=(vector, vector, vector, vector, P(), P("row", "col")),
        out_specs=(vector, vector, P()),
        check_vma=False,
    )
```

```python
import functools

import jax
import jax.numpy as jnp
from jax import lax
from jax.experimental import pallas as pl
from jax.experimental.pallas import tpu as pltpu
from jax.sharding import PartitionSpec as P

LOGICAL = pl.DeviceIdType.LOGICAL
LANES = 128
LAYERS = 4
UNROLL_MOST = 32
SMALLEST_SQUARE = 1e-12


def each(count, body):
    if count <= UNROLL_MOST:
        for i in range(count):
            body(i)
    else:
        lax.fori_loop(0, count, lambda i, carry: (body(i), carry)[1], 0)


def arrived(ref, count, sem):
    part = ref.at[pl.ds(0, count)]
    pltpu.make_async_copy(part, part, sem).wait()


def kernel(
    rows_count,
    cols_count,
    right_in,
    left_in,
    prev_right_in,
    prev_left_in,
    coupling_in,
    ladder_in,
    next_right_out,
    next_left_out,
    coefficients_out,
    vectors_own,
    coupling_own,
    ladder_own,
    left_sent,
    mates_sent,
    right_got,
    left_got,
    mates_got,
    right_part,
    left_part,
    right_part_got,
    left_part_got,
    sums_sent,
    sums_got,
    load_sem,
    send_sem,
    recv_sem,
):
    devices = rows_count * cols_count
    depth, share = right_in.shape
    pack = LANES // share
    pairs_total = share * devices
    my_row = lax.axis_index("row")
    my_col = lax.axis_index("col")
    me = my_row * cols_count + my_col
    home_col = lax.div(me, rows_count)
    home_slot = lax.rem(me, rows_count)
    at_home = home_col == my_col

    layers = LAYERS if rows_count % LAYERS == 0 else 1
    span = rows_count // layers
    layer = lax.div(my_row, span)
    above = layer > lax.div(lax.div(my_col * rows_count, cols_count), span)
    first_half = my_row < rows_count // 2

    groups = devices // pack
    my_group = lax.div(me, pack)
    my_sub = lax.rem(me, pack)
    loads = [
        pltpu.make_async_copy(src, dst, load_sem.at[i])
        for i, (src, dst) in enumerate(
            (
                (right_in, vectors_own.at[0]),
                (left_in, vectors_own.at[1]),
                (prev_right_in, vectors_own.at[2]),
                (prev_left_in, vectors_own.at[3]),
                (coupling_in, coupling_own),
                (ladder_in, ladder_own),
            )
        )
    ]
    row_start = my_row * cols_count

    def peer(i):
        return row_start + lax.rem(my_col + i + 1, cols_count)

    def holder(i):
        return my_col * rows_count + lax.rem(home_slot + i, rows_count)

    def user(i):
        step = jnp.where(first_half, rows_count - i, i)
        return lax.rem(my_row + step, rows_count) * cols_count + home_col

    def unless_me(i, go):
        if i == 0:
            pl.when(jnp.logical_not(at_home))(go)
        else:
            go()

    barrier = pltpu.get_barrier_semaphore()

    def greet(device):
        pl.semaphore_signal(barrier, inc=1, device_id=device, device_id_type=LOGICAL)

    for load in loads[:2]:
        load.start()
    for i in range(rows_count):
        unless_me(i, lambda: greet(holder(i)))
    for i in range(cols_count - 1):
        greet(peer(i))
    for row in range(span, rows_count):
        pl.when(row >= (layer + 1) * span)(
            functools.partial(greet, row * cols_count + home_col)
        )
    for load in loads[2:]:
        load.start()

    lane = lax.broadcasted_iota(jnp.int32, (depth, LANES), 1)
    sub = lax.broadcasted_iota(jnp.int32, (depth, LANES), 0)

    mine = lane // share == my_sub

    def spread(i):
        return jnp.where(mine, jnp.concatenate([vectors_own[i]] * pack, axis=1), 0.0)

    def to_lanes(columns):
        row = jnp.zeros((depth, LANES), jnp.float32)
        for i, column in enumerate(columns):
            row = row + jnp.where(lane == sub + i * depth, column, 0.0)
        return jnp.sum(row, axis=0, keepdims=True)

    def to_column(row, i):
        return jnp.sum(jnp.where(lane == sub + i * depth, row, 0.0), axis=1, keepdims=True)

    for load in loads[:2]:
        load.wait()
    right_own = spread(0)
    left_own = spread(1)
    mates_sent[0] = right_own
    left_sent[0] = left_own
    left_got[pl.ds(my_col, 1)] = left_own[None]

    @pl.when(at_home)
    def _():
        right_got[pl.ds(home_slot, 1)] = right_own[None]

    awaited = rows_count + cols_count - 1 - at_home.astype(jnp.int32)
    pl.semaphore_wait(barrier, awaited + jnp.where(above, rows_count, 0))

    def send(src, dst, sems, device):
        pltpu.make_async_remote_copy(
            src_ref=src,
            dst_ref=dst,
            send_sem=send_sem.at[sems],
            recv_sem=recv_sem.at[sems],
            device_id=device,
            device_id_type=LOGICAL,
        ).start()

    def send_right(i):
        unless_me(i, lambda: send(mates_sent.at[0], right_got.at[home_slot], 0, user(i)))

    for i in range(1, rows_count // 2):
        send_right(i)
    for i in range(cols_count - 1):
        send(left_sent.at[0], left_got.at[my_col], 1, peer(i))
    for i in (*range(rows_count // 2, rows_count), 0):
        send_right(i)

    for load in loads[2:]:
        load.wait()
    mates_sent[1] = spread(2)
    mates_sent[2] = spread(3)
    mates_got[pl.ds(my_sub, 1)] = mates_sent[...][None]
    coupling_row = coupling_own[...]
    near = lax.broadcasted_iota(jnp.int32, (depth, depth), 0) == lax.broadcasted_iota(
        jnp.int32, (depth, depth), 1
    )

    def coefficient(i):
        return jnp.sum(jnp.where(near, coupling_row[i : i + 1], 0.0), axis=1, keepdims=True)

    def joined(ref, count):
        return jnp.concatenate(
            [sum(ref[i * pack + j] for j in range(pack)) for i in range(count // pack)], axis=1
        )

    arrived(left_got, cols_count - 1, recv_sem.at[1])
    left_rows = joined(left_got, cols_count)
    left_terms = jnp.dot(
        left_rows.astype(jnp.bfloat16), ladder_own[...], preferred_element_type=jnp.float32
    )
    for i in range(rows_count // pack):
        left_part[i] = left_terms[:, i * LANES : (i + 1) * LANES]

    def send_left_parts():
        for i in (*range(1, rows_count), 0):
            chunk = lax.div(lax.rem(home_slot + i, rows_count), pack)
            unless_me(
                i, lambda: send(left_part.at[chunk], left_part_got.at[my_row], 2, holder(i))
            )

    pl.when(above)(send_left_parts)
    for i in range(pack - 1):
        mate = me - my_sub + lax.rem(my_sub + i + 1, pack)
        send(mates_sent, mates_got.at[my_sub], 5, mate)

    @pl.when(at_home)
    def _():
        left_part_got[pl.ds(my_row, 1)] = left_part[pl.ds(lax.div(home_slot, pack), 1)]
        arrived(right_got, rows_count - 1, recv_sem.at[0])

    @pl.when(jnp.logical_not(at_home))
    def _():
        arrived(right_got, rows_count, recv_sem.at[0])

    pl.when(jnp.logical_not(above))(send_left_parts)
    right_cols = joined(right_got, rows_count)
    right_terms = lax.dot_general(
        right_cols.astype(jnp.bfloat16),
        ladder_own[...],
        (((1,), (1,)), ((), ())),
        preferred_element_type=jnp.float32,
    )
    for i in range(cols_count // pack):
        right_part[i] = right_terms[:, i * LANES : (i + 1) * LANES]

    for i in range(cols_count - 1):
        chunk = lax.div(lax.rem(my_col + i + 1, cols_count), pack)
        send(right_part.at[chunk], right_part_got.at[my_col], 3, peer(i))
    right_part_got[pl.ds(my_col, 1)] = right_part[pl.ds(lax.div(my_col, pack), 1)]

    def inner(first, second):
        return jnp.sum(first * second, axis=1, keepdims=True)

    def inverse(square):
        usable = square > SMALLEST_SQUARE
        return jnp.where(usable, 1.0 / jnp.where(usable, square, 1.0), 0.0)

    arrived(mates_got, pack - 1, recv_sem.at[5])
    right, prev_right, prev_left = (
        sum(mates_got[i, j] for i in range(pack)) for j in range(3)
    )
    first_col = my_col - my_sub
    left = sum(left_got[first_col + i] for i in range(pack))
    right_square = inner(right, right)
    left_square = inner(left, left)
    left_right = inner(left, right)
    right_inverse = inverse(right_square)
    left_inverse = inverse(left_square)

    arrived(right_part_got, cols_count - 1, recv_sem.at[3])
    image_right = jnp.sum(right_part_got[...], axis=0)
    alpha_part = inner(left, image_right)
    right_base = image_right - coefficient(1) * prev_right
    right_fit = inner(right_base, right) * right_inverse
    right_rest = right_base - right_fit * right

    @pl.when(at_home)
    def _():
        arrived(left_part_got, rows_count - 1, recv_sem.at[2])

    @pl.when(jnp.logical_not(at_home))
    def _():
        arrived(left_part_got, rows_count, recv_sem.at[2])

    left_base = jnp.sum(left_part_got[...], axis=0) - coefficient(0) * prev_left
    left_fit = inner(left_base, left) * left_inverse
    left_rest = left_base - left_fit * left

    sums_sent[...] = to_lanes(
        [
            alpha_part,
            right_fit,
            left_fit,
            inner(right_rest, right_rest),
            inner(right_rest, right),
            right_square,
            inner(left_rest, left_rest),
            inner(left_rest, left),
            left_square,
            inner(left_rest, right_rest),
            inner(left_rest, right),
            inner(left, right_rest),
            left_right,
        ]
    )
    low = my_group < groups // 2

    def far_first(i):
        down = groups - 1 - i
        down = down - (down <= my_group).astype(jnp.int32)
        up = i + (i >= my_group).astype(jnp.int32)
        return jnp.where(low, down, up) * pack + my_sub

    each(
        groups - 1,
        lambda i: send(sums_sent, sums_got.at[pl.ds(my_group, 1)], 4, far_first(i)),
    )
    sums_got[pl.ds(my_group, 1)] = sums_sent[...]

    arrived(right_got, rows_count - 1, send_sem.at[0])
    arrived(left_got, cols_count - 1, send_sem.at[1])
    arrived(left_part_got, rows_count - 1, send_sem.at[2])
    arrived(right_part_got, cols_count - 1, send_sem.at[3])
    arrived(mates_got, pack - 1, send_sem.at[5])

    @pl.when(jnp.logical_not(at_home))
    def _():
        arrived(right_got, 1, send_sem.at[0])
        arrived(left_part_got, 1, send_sem.at[2])

    arrived(sums_got, groups - 1, recv_sem.at[4])
    sums = sums_got[...]

    def value(i):
        return pltpu.roll(sums, LANES - i * depth, 1)

    def total(values):
        return jnp.sum(values, axis=0, keepdims=True) / pairs_total

    alpha_row = total(sums)
    right_off = value(1) - alpha_row
    left_off = value(2) - alpha_row
    right_norm = to_column(
        total(value(3) + right_off * (2.0 * value(4) + right_off * value(5))), 0
    )
    left_norm = to_column(total(value(6) + left_off * (2.0 * value(7) + left_off * value(8))), 0)
    omega_val = to_column(
        total(
            value(9)
            + right_off * value(10)
            + left_off * value(11)
            + right_off * left_off * value(12)
        ),
        0,
    )
    alpha_now = to_column(alpha_row, 0)
    right_res = right_base - alpha_now * right
    left_res = left_base - alpha_now * left
    safe_omega = jnp.maximum(jnp.abs(omega_val), 0.1 * jnp.sqrt(right_norm * left_norm + 1e-06))
    beta_new = jnp.sqrt(safe_omega)
    gamma_new = omega_val / beta_new

    def own_part(array):
        out = array[:, :share]
        for i in range(1, pack):
            out = jnp.where(
                my_sub == i, array[:, i * share : (i + 1) * share], out
            )
        return out

    next_right_out[...] = own_part(right_res / beta_new)
    next_left_out[...] = own_part(left_res * (gamma_new / safe_omega))
    coefficients_out[0:1] = alpha_row[:, :depth]
    coefficients_out[1:2] = to_lanes([beta_new])[:, :depth]
    coefficients_out[2:3] = to_lanes([gamma_new])[:, :depth]
    arrived(sums_got, groups - 1, send_sem.at[4])


def store(a_in, b_in, c_in, a_out, b_out, c_out, sem):
    copies = [
        pltpu.make_async_copy(src, dst, sem.at[i])
        for i, (src, dst) in enumerate(((a_in, a_out), (b_in, b_out), (c_in, c_out)))
    ]
    for copy in copies:
        copy.start()
    for copy in copies:
        copy.wait()


def local(rows_count, cols_count, right, left, prev_right, prev_left, coupling, ladder):
    depth, share = right.shape
    devices = rows_count * cols_count
    pack = LANES // share
    f32 = jnp.float32

    def tiles(count):
        return pltpu.VMEM((count, depth, LANES), f32)

    results = pl.pallas_call(
        functools.partial(kernel, rows_count, cols_count),
        out_shape=(
            pltpu.VMEM(right.shape, f32),
            pltpu.VMEM(left.shape, f32),
            pltpu.VMEM((3, depth), f32),
        ),
        in_specs=[pl.BlockSpec(memory_space=pltpu.HBM)] * 6,
        out_specs=(pl.BlockSpec(memory_space=pltpu.VMEM),) * 3,
        scratch_shapes=[
            pltpu.VMEM((4, depth, share), f32),
            pltpu.VMEM(coupling.shape, f32),
            pltpu.VMEM(ladder.shape, ladder.dtype),
            tiles(1),
            tiles(3),
            tiles(rows_count),
            tiles(cols_count),
            pltpu.VMEM((pack, 3, depth, LANES), f32),
            tiles(cols_count // pack),
            tiles(rows_count // pack),
            tiles(cols_count),
            tiles(rows_count),
            pltpu.VMEM((1, LANES), f32),
            pltpu.VMEM((devices // pack, LANES), f32),
            pltpu.SemaphoreType.DMA((6,)),
            pltpu.SemaphoreType.DMA((6,)),
            pltpu.SemaphoreType.DMA((6,)),
        ],
        compiler_params=pltpu.CompilerParams(
            collective_id=0, has_side_effects=True, vmem_limit_bytes=32 * 1024 * 1024
        ),
    )(*(pltpu.with_memory_space_constraint(x, pltpu.HBM) for x in (right, left, prev_right, prev_left, coupling, ladder)))
    return pl.pallas_call(
        store,
        out_shape=tuple(jax.ShapeDtypeStruct(x.shape, x.dtype) for x in results),
        in_specs=[pl.BlockSpec(memory_space=pltpu.VMEM)] * 3,
        out_specs=(pl.BlockSpec(memory_space=pltpu.HBM),) * 3,
        scratch_shapes=[pltpu.SemaphoreType.DMA((3,))],
        compiler_params=pltpu.CompilerParams(vmem_limit_bytes=1024 * 1024),
    )(*(pltpu.with_memory_space_constraint(x, pltpu.VMEM) for x in results))


def solution(mesh):
    vector = P(None, ("row", "col"))
    return jax.shard_map(
        functools.partial(local, mesh.shape["row"], mesh.shape["col"]),
        mesh=mesh,
        in_specs=(vector, vector, vector, vector, P(), P("row", "col")),
        out_specs=(vector, vector, P()),
        check_vma=False,
    )
```

```python
import functools

import jax
import jax.numpy as jnp
from jax import lax
from jax.experimental import pallas as pl
from jax.experimental.pallas import tpu as pltpu
from jax.sharding import PartitionSpec as P

LOGICAL = pl.DeviceIdType.LOGICAL
LANES = 128
LAYERS = 4
UNROLL_MOST = 32
SMALLEST_SQUARE = 1e-12


def each(count, body):
    if count <= UNROLL_MOST:
        for i in range(count):
            body(i)
    else:
        lax.fori_loop(0, count, lambda i, carry: (body(i), carry)[1], 0)


def arrived(ref, count, sem):
    part = ref.at[pl.ds(0, count)]
    pltpu.make_async_copy(part, part, sem).wait()


def kernel(
    rows_count,
    cols_count,
    right_in,
    left_in,
    prev_right_in,
    prev_left_in,
    coupling_in,
    ladder_in,
    next_right_out,
    next_left_out,
    coefficients_out,
    vectors_own,
    coupling_own,
    ladder_own,
    left_sent,
    mates_sent,
    right_got,
    left_got,
    mates_got,
    right_part,
    left_part,
    right_part_got,
    left_part_got,
    sums_sent,
    sums_got,
    load_sem,
    send_sem,
    recv_sem,
):
    devices = rows_count * cols_count
    depth, share = right_in.shape
    pack = LANES // share
    pairs_total = share * devices
    my_row = lax.axis_index("row")
    my_col = lax.axis_index("col")
    me = my_row * cols_count + my_col
    home_col = lax.div(me, rows_count)
    home_slot = lax.rem(me, rows_count)
    at_home = home_col == my_col

    layers = LAYERS if rows_count % LAYERS == 0 else 1
    span = rows_count // layers
    layer = lax.div(my_row, span)
    below = layer < lax.div(lax.div(my_col * rows_count, cols_count), span)
    first_half = my_row < rows_count // 2

    groups = devices // pack
    my_group = lax.div(me, pack)
    my_sub = lax.rem(me, pack)
    loads = [
        pltpu.make_async_copy(src, dst, load_sem.at[i])
        for i, (src, dst) in enumerate(
            (
                (right_in, vectors_own.at[0]),
                (left_in, vectors_own.at[1]),
                (prev_right_in, vectors_own.at[2]),
                (prev_left_in, vectors_own.at[3]),
                (coupling_in, coupling_own),
                (ladder_in, ladder_own),
            )
        )
    ]
    row_start = my_row * cols_count

    def peer(i):
        return row_start + lax.rem(my_col + i + 1, cols_count)

    def holder(i):
        return my_col * rows_count + lax.rem(home_slot + i, rows_count)

    def user(i):
        step = jnp.where(first_half, rows_count - i, i)
        return lax.rem(my_row + step, rows_count) * cols_count + home_col

    def unless_me(i, go):
        if i == 0:
            pl.when(jnp.logical_not(at_home))(go)
        else:
            go()

    barrier = pltpu.get_barrier_semaphore()

    def greet(device):
        pl.semaphore_signal(barrier, inc=1, device_id=device, device_id_type=LOGICAL)

    for load in loads[:2]:
        load.start()
    for i in range(cols_count - 1):
        greet(peer(i))
    for i in range(rows_count):
        unless_me(i, lambda: greet(holder(i)))
    for row in range(rows_count):
        is_me = jnp.logical_and(at_home, my_row == row)
        pl.when(jnp.logical_and(row >= layer * span, jnp.logical_not(is_me)))(
            functools.partial(greet, row * cols_count + home_col)
        )
    for load in loads[2:]:
        load.start()

    lane = lax.broadcasted_iota(jnp.int32, (depth, LANES), 1)
    sub = lax.broadcasted_iota(jnp.int32, (depth, LANES), 0)

    mine = lane // share == my_sub

    def spread(i):
        return jnp.where(mine, jnp.concatenate([vectors_own[i]] * pack, axis=1), 0.0)

    def to_lanes(columns):
        row = jnp.zeros((depth, LANES), jnp.float32)
        for i, column in enumerate(columns):
            row = row + jnp.where(lane == sub + i * depth, column, 0.0)
        return jnp.sum(row, axis=0, keepdims=True)

    def to_column(row, i):
        return jnp.sum(jnp.where(lane == sub + i * depth, row, 0.0), axis=1, keepdims=True)

    for load in loads[:2]:
        load.wait()
    right_own = spread(0)
    left_own = spread(1)
    mates_sent[0] = right_own
    left_sent[0] = left_own
    left_got[pl.ds(my_col, 1)] = left_own[None]

    @pl.when(at_home)
    def _():
        right_got[pl.ds(home_slot, 1)] = right_own[None]

    others = rows_count - at_home.astype(jnp.int32)
    pl.semaphore_wait(barrier, cols_count - 1 + others + jnp.where(below, 0, others))

    def send(src, dst, sems, device):
        pltpu.make_async_remote_copy(
            src_ref=src,
            dst_ref=dst,
            send_sem=send_sem.at[sems],
            recv_sem=recv_sem.at[sems],
            device_id=device,
            device_id_type=LOGICAL,
        ).start()

    def send_right(i):
        unless_me(i, lambda: send(mates_sent.at[0], right_got.at[home_slot], 0, user(i)))

    for i in range(cols_count - 1):
        send(left_sent.at[0], left_got.at[my_col], 1, peer(i))
    for i in (*range(1, rows_count), 0):
        send_right(i)

    for load in loads[2:]:
        load.wait()
    mates_sent[1] = spread(2)
    mates_sent[2] = spread(3)
    mates_got[pl.ds(my_sub, 1)] = mates_sent[...][None]
    coupling_row = coupling_own[...]
    near = lax.broadcasted_iota(jnp.int32, (depth, depth), 0) == lax.broadcasted_iota(
        jnp.int32, (depth, depth), 1
    )

    def coefficient(i):
        return jnp.sum(jnp.where(near, coupling_row[i : i + 1], 0.0), axis=1, keepdims=True)

    def joined(ref, count):
        return jnp.concatenate(
            [sum(ref[i * pack + j] for j in range(pack)) for i in range(count // pack)], axis=1
        )

    arrived(left_got, cols_count - 1, recv_sem.at[1])
    left_rows = joined(left_got, cols_count)
    left_terms = jnp.dot(
        left_rows.astype(jnp.bfloat16), ladder_own[...], preferred_element_type=jnp.float32
    )
    for i in range(rows_count // pack):
        left_part[i] = left_terms[:, i * LANES : (i + 1) * LANES]

    def send_left_parts():
        for i in (*range(1, rows_count), 0):
            chunk = lax.div(lax.rem(home_slot + i, rows_count), pack)
            unless_me(
                i, lambda: send(left_part.at[chunk], left_part_got.at[my_row], 2, holder(i))
            )

    pl.when(jnp.logical_not(below))(send_left_parts)
    for i in range(pack - 1):
        mate = me - my_sub + lax.rem(my_sub + i + 1, pack)
        send(mates_sent, mates_got.at[my_sub], 5, mate)

    @pl.when(at_home)
    def _():
        left_part_got[pl.ds(my_row, 1)] = left_part[pl.ds(lax.div(home_slot, pack), 1)]
        arrived(right_got, rows_count - 1, recv_sem.at[0])

    @pl.when(jnp.logical_not(at_home))
    def _():
        arrived(right_got, rows_count, recv_sem.at[0])

    pl.when(below)(send_left_parts)
    right_cols = joined(right_got, rows_count)
    right_terms = lax.dot_general(
        right_cols.astype(jnp.bfloat16),
        ladder_own[...],
        (((1,), (1,)), ((), ())),
        preferred_element_type=jnp.float32,
    )
    for i in range(cols_count // pack):
        right_part[i] = right_terms[:, i * LANES : (i + 1) * LANES]

    for i in range(cols_count - 1):
        chunk = lax.div(lax.rem(my_col + i + 1, cols_count), pack)
        send(right_part.at[chunk], right_part_got.at[my_col], 3, peer(i))
    right_part_got[pl.ds(my_col, 1)] = right_part[pl.ds(lax.div(my_col, pack), 1)]

    def inner(first, second):
        return jnp.sum(first * second, axis=1, keepdims=True)

    def inverse(square):
        usable = square > SMALLEST_SQUARE
        return jnp.where(usable, 1.0 / jnp.where(usable, square, 1.0), 0.0)

    arrived(mates_got, pack - 1, recv_sem.at[5])
    right, prev_right, prev_left = (
        sum(mates_got[i, j] for i in range(pack)) for j in range(3)
    )
    first_col = my_col - my_sub
    left = sum(left_got[first_col + i] for i in range(pack))
    right_square = inner(right, right)
    left_square = inner(left, left)
    left_right = inner(left, right)
    right_inverse = inverse(right_square)
    left_inverse = inverse(left_square)

    arrived(right_part_got, cols_count - 1, recv_sem.at[3])
    image_right = jnp.sum(right_part_got[...], axis=0)
    alpha_part = inner(left, image_right)
    right_base = image_right - coefficient(1) * prev_right
    right_fit = inner(right_base, right) * right_inverse
    right_rest = right_base - right_fit * right

    @pl.when(at_home)
    def _():
        arrived(left_part_got, rows_count - 1, recv_sem.at[2])

    @pl.when(jnp.logical_not(at_home))
    def _():
        arrived(left_part_got, rows_count, recv_sem.at[2])

    left_base = jnp.sum(left_part_got[...], axis=0) - coefficient(0) * prev_left
    left_fit = inner(left_base, left) * left_inverse
    left_rest = left_base - left_fit * left

    sums_sent[...] = to_lanes(
        [
            alpha_part,
            right_fit,
            left_fit,
            inner(right_rest, right_rest),
            inner(right_rest, right),
            right_square,
            inner(left_rest, left_rest),
            inner(left_rest, left),
            left_square,
            inner(left_rest, right_rest),
            inner(left_rest, right),
            inner(left, right_rest),
            left_right,
        ]
    )
    low = my_group < groups // 2

    def far_first(i):
        down = groups - 1 - i
        down = down - (down <= my_group).astype(jnp.int32)
        up = i + (i >= my_group).astype(jnp.int32)
        return jnp.where(low, down, up) * pack + my_sub

    each(
        groups - 1,
        lambda i: send(sums_sent, sums_got.at[pl.ds(my_group, 1)], 4, far_first(i)),
    )
    sums_got[pl.ds(my_group, 1)] = sums_sent[...]

    arrived(right_got, rows_count - 1, send_sem.at[0])
    arrived(left_got, cols_count - 1, send_sem.at[1])
    arrived(left_part_got, rows_count - 1, send_sem.at[2])
    arrived(right_part_got, cols_count - 1, send_sem.at[3])
    arrived(mates_got, pack - 1, send_sem.at[5])

    @pl.when(jnp.logical_not(at_home))
    def _():
        arrived(right_got, 1, send_sem.at[0])
        arrived(left_part_got, 1, send_sem.at[2])

    arrived(sums_got, groups - 1, recv_sem.at[4])
    sums = sums_got[...]

    def value(i):
        return pltpu.roll(sums, LANES - i * depth, 1)

    def total(values):
        return jnp.sum(values, axis=0, keepdims=True) / pairs_total

    alpha_row = total(sums)
    right_off = value(1) - alpha_row
    left_off = value(2) - alpha_row
    right_norm = to_column(
        total(value(3) + right_off * (2.0 * value(4) + right_off * value(5))), 0
    )
    left_norm = to_column(total(value(6) + left_off * (2.0 * value(7) + left_off * value(8))), 0)
    omega_val = to_column(
        total(
            value(9)
            + right_off * value(10)
            + left_off * value(11)
            + right_off * left_off * value(12)
        ),
        0,
    )
    alpha_now = to_column(alpha_row, 0)
    right_res = right_base - alpha_now * right
    left_res = left_base - alpha_now * left
    safe_omega = jnp.maximum(jnp.abs(omega_val), 0.1 * jnp.sqrt(right_norm * left_norm + 1e-06))
    beta_new = jnp.sqrt(safe_omega)
    gamma_new = omega_val / beta_new

    def own_part(array):
        out = array[:, :share]
        for i in range(1, pack):
            out = jnp.where(
                my_sub == i, array[:, i * share : (i + 1) * share], out
            )
        return out

    next_right_out[...] = own_part(right_res / beta_new)
    next_left_out[...] = own_part(left_res * (gamma_new / safe_omega))
    coefficients_out[0:1] = alpha_row[:, :depth]
    coefficients_out[1:2] = to_lanes([beta_new])[:, :depth]
    coefficients_out[2:3] = to_lanes([gamma_new])[:, :depth]
    arrived(sums_got, groups - 1, send_sem.at[4])


def store(a_in, b_in, c_in, a_out, b_out, c_out, sem):
    copies = [
        pltpu.make_async_copy(src, dst, sem.at[i])
        for i, (src, dst) in enumerate(((a_in, a_out), (b_in, b_out), (c_in, c_out)))
    ]
    for copy in copies:
        copy.start()
    for copy in copies:
        copy.wait()


def local(rows_count, cols_count, right, left, prev_right, prev_left, coupling, ladder):
    depth, share = right.shape
    devices = rows_count * cols_count
    pack = LANES // share
    f32 = jnp.float32

    def tiles(count):
        return pltpu.VMEM((count, depth, LANES), f32)

    results = pl.pallas_call(
        functools.partial(kernel, rows_count, cols_count),
        out_shape=(
            pltpu.VMEM(right.shape, f32),
            pltpu.VMEM(left.shape, f32),
            pltpu.VMEM((3, depth), f32),
        ),
        in_specs=[pl.BlockSpec(memory_space=pltpu.HBM)] * 6,
        out_specs=(pl.BlockSpec(memory_space=pltpu.VMEM),) * 3,
        scratch_shapes=[
            pltpu.VMEM((4, depth, share), f32),
            pltpu.VMEM(coupling.shape, f32),
            pltpu.VMEM(ladder.shape, ladder.dtype),
            tiles(1),
            tiles(3),
            tiles(rows_count),
            tiles(cols_count),
            pltpu.VMEM((pack, 3, depth, LANES), f32),
            tiles(cols_count // pack),
            tiles(rows_count // pack),
            tiles(cols_count),
            tiles(rows_count),
            pltpu.VMEM((1, LANES), f32),
            pltpu.VMEM((devices // pack, LANES), f32),
            pltpu.SemaphoreType.DMA((6,)),
            pltpu.SemaphoreType.DMA((6,)),
            pltpu.SemaphoreType.DMA((6,)),
        ],
        compiler_params=pltpu.CompilerParams(
            collective_id=0, has_side_effects=True, vmem_limit_bytes=32 * 1024 * 1024
        ),
    )(*(pltpu.with_memory_space_constraint(x, pltpu.HBM) for x in (right, left, prev_right, prev_left, coupling, ladder)))
    return pl.pallas_call(
        store,
        out_shape=tuple(jax.ShapeDtypeStruct(x.shape, x.dtype) for x in results),
        in_specs=[pl.BlockSpec(memory_space=pltpu.VMEM)] * 3,
        out_specs=(pl.BlockSpec(memory_space=pltpu.HBM),) * 3,
        scratch_shapes=[pltpu.SemaphoreType.DMA((3,))],
        compiler_params=pltpu.CompilerParams(vmem_limit_bytes=1024 * 1024),
    )(*(pltpu.with_memory_space_constraint(x, pltpu.VMEM) for x in results))


def solution(mesh):
    vector = P(None, ("row", "col"))
    return jax.shard_map(
        functools.partial(local, mesh.shape["row"], mesh.shape["col"]),
        mesh=mesh,
        in_specs=(vector, vector, vector, vector, P(), P("row", "col")),
        out_specs=(vector, vector, P()),
        check_vma=False,
    )
```
